128 devices in a mesh: section: 8 (over z, core), head: 16 (over x, y).
Axes of the slice: x: 4, y: 4, z: 4, core: 2. Of those that a mesh axis runs over, the one named last changes fastest.
Arguments:
- latents: bfloat16 [4, 256, 3072], P(None, 'head'), may hold values from -6 to 6
- patch_numbers: int32 [3], replicated, may hold values from 0 to 3
- prior_step_cache: bfloat16 [8, 16, 256, 2, 2048], P('section', None, 'head'), may hold values from -6 to 6
- old_block_index: int32 [8, 3, 4], P('section'), may hold values from 0 to 15
- modulation_offset: float32 [8, 3072], P('section'), may hold values from -3 to 3
- modulation_scale: float32 [8, 3072], P('section'), may hold values from -3 to 3
- modulation_gate: float32 [8, 3072], P('section'), may hold values from 0.5 to 1.5
- query_key_value_weight: bfloat16 [8, 3072, 3, 2048], P('section', None, None, 'head'), may hold values from -0.109375 to 0.109375
- feedforward_input_weight: bfloat16 [8, 3072, 12288], P('section', None, 'head'), may hold values from -0.109375 to 0.109375
- adapter_down_weight: bfloat16 [8, 3072, 64], P('section'), may hold values from -0.109375 to 0.109375
- adapter_up_query_key_value: bfloat16 [8, 64, 3, 2048], P('section', None, None, 'head'), may hold values from -0.75 to 0.75
- adapter_up_feedforward: bfloat16 [8, 64, 12288], P('section', None, 'head'), may hold values from -0.75 to 0.75
- attention_output_weight: bfloat16 [8, 2048, 3072], P('section', 'head'), may hold values from -0.5 to 0.5
- feedforward_output_weight: bfloat16 [8, 12288, 3072], P('section', 'head'), may hold values from -0.0546875 to 0.0546875
Outputs:
- hidden: bfloat16 [8, 3, 256, 3072], P('section', None, 'head')
The draws below stay inside these ranges and needn't reach their ends.
All inputs are finite; a program needn't handle non-finite values.
Results may differ from the reference program's by a relative error of at most 0.033.
Values may be sent and summed in bfloat16 or wider, within the bound.
A program may use at most 128 MiB of HBM per device.

```python
import math
import jax
import jax.numpy as jnp
from jax import lax

MODEL_WIDTH = 3072
FEEDFWD_HIDDEN = 12288
DH = 128
HEADS = 16
ADAPTER_RANK = 64
PATCHES = 3
POOL = 4
BLK = 256
NBLK = 16
NSEL = 4
ATTENTION_WIDTH = 2048
PTOK = 256
LAYER_COUNT = 8
N_HEAD = 16


def place_ends(entries, rng, least, top_value):
    place = [jax.random.randint(jax.random.fold_in(rng, axis), (), 0, length) for axis, length in enumerate(entries.shape)]
    longest = entries.shape.index(max(entries.shape))
    neighbour = place[:longest] + [(place[longest] + 1) % entries.shape[longest]] + place[longest + 1:]
    return entries.at[tuple(place)].set(least).at[tuple(neighbour)].set(top_value)


def steps_of(key, extent, cuts, smallest, largest):
    gain, own = 1.0, jax.random.fold_in(key, 6)
    for position, shards_of in cuts:
        steps = jnp.exp(jax.random.uniform(jax.random.fold_in(own, position), (shards_of,), jnp.float32, smallest / len(cuts), largest / len(cuts)))
        gain = gain * jnp.repeat(steps, extent[position] // shards_of).reshape([-1 if axis == position else 1 for axis in range(len(extent))])
    return gain


def bell_draw(rng, extent, scale, reach, cuts=(), kind=jnp.bfloat16):
    drawn = jax.random.normal(rng, extent, jnp.float32) * scale
    if len(cuts) > 0:
        drawn = steps_of(rng, extent, cuts, -0.22, 0.18) * drawn
    return jnp.clip(drawn, min=-reach, max=reach).astype(kind)


def setup_inputs(seed: int = 0) -> dict:
    key_of = jax.random.split(jax.random.key(seed), 15)
    return {
        "latents": bell_draw(key_of[0], (POOL, PTOK, MODEL_WIDTH), 1.0, 6.0, ((1, 16),)),
        "patch_numbers": jax.random.randint(key_of[1], (PATCHES,), 0, POOL).astype(jnp.int32),
        "prior_step_cache": bell_draw(key_of[2], (LAYER_COUNT, NBLK, BLK, 2, ATTENTION_WIDTH), 1.0, 6.0, ((0, 8), (2, 16))),
        "old_block_index": place_ends(jax.random.randint(key_of[3], (LAYER_COUNT, PATCHES, NSEL), 0, NBLK), jax.random.fold_in(key_of[3], 1), 0, NBLK - 1).astype(jnp.int32),
        "modulation_offset": bell_draw(key_of[4], (LAYER_COUNT, MODEL_WIDTH), 0.5, 3.0, ((0, 8),), jnp.float32),
        "modulation_scale": bell_draw(key_of[5], (LAYER_COUNT, MODEL_WIDTH), 0.5, 3.0, ((0, 8),), jnp.float32),
        "modulation_gate": jnp.clip(0.5 + 1.0 * jax.random.uniform(key_of[6], (LAYER_COUNT, MODEL_WIDTH), jnp.float32) ** steps_of(key_of[6], (LAYER_COUNT, MODEL_WIDTH), ((0, 8),), -0.2, 0.2), 0.5, 1.5),
        "query_key_value_weight": bell_draw(key_of[7], (LAYER_COUNT, MODEL_WIDTH, 3, ATTENTION_WIDTH), MODEL_WIDTH ** -0.5, 0.109375, ((0, 8), (3, 16))),
        "feedforward_input_weight": bell_draw(key_of[8], (LAYER_COUNT, MODEL_WIDTH, FEEDFWD_HIDDEN), MODEL_WIDTH ** -0.5, 0.109375, ((0, 8), (2, 16))),
        "adapter_down_weight": bell_draw(key_of[9], (LAYER_COUNT, MODEL_WIDTH, ADAPTER_RANK), MODEL_WIDTH ** -0.5, 0.109375, ((0, 8),)),
        "adapter_up_query_key_value": bell_draw(key_of[10], (LAYER_COUNT, ADAPTER_RANK, 3, ATTENTION_WIDTH), ADAPTER_RANK ** -0.5, 0.75, ((0, 8), (3, 16))),
        "adapter_up_feedforward": bell_draw(key_of[11], (LAYER_COUNT, ADAPTER_RANK, FEEDFWD_HIDDEN), ADAPTER_RANK ** -0.5, 0.75, ((0, 8), (2, 16))),
        "attention_output_weight": bell_draw(key_of[12], (LAYER_COUNT, ATTENTION_WIDTH, MODEL_WIDTH), (ATTENTION_WIDTH // 16) ** -0.5, 0.5, ((0, 8), (1, 16))),
        "feedforward_output_weight": bell_draw(key_of[13], (LAYER_COUNT, FEEDFWD_HIDDEN, MODEL_WIDTH), FEEDFWD_HIDDEN ** -0.5, 0.0546875, ((0, 8), (1, 16))),
    }


def modulate(resid, shift, scale):
    values = resid.astype(jnp.float32)
    center = values - lax.optimization_barrier(jnp.mean(values, axis=-1, keepdims=True))
    spread = lax.optimization_barrier(jnp.mean(center * center, axis=-1, keepdims=True))
    normed = center * lax.rsqrt(spread + 1e-06)
    return (normed * (1.0 + scale) + shift).astype(jnp.bfloat16)

def rms_unit(values):
    return values * lax.rsqrt(lax.optimization_barrier(jnp.mean(values * values, axis=-1, keepdims=True)) + 1e-06)

def single_layer_body(resid, blocks, cache, shift, scale, gate, w_attn, w_ffn, down_product, adapter_attention_up, adapter_feedforward_up, out_attn, out_ffn):
    modded = modulate(resid, shift, scale)
    lowrank = jnp.dot(modded, down_product, preferred_element_type=jnp.float32).astype(jnp.bfloat16)
    qkv = jnp.dot(modded, w_attn.reshape(MODEL_WIDTH, 3 * ATTENTION_WIDTH), preferred_element_type=jnp.float32)
    qkv = qkv + jnp.dot(lowrank, adapter_attention_up.reshape(ADAPTER_RANK, 3 * ATTENTION_WIDTH), preferred_element_type=jnp.float32)
    pre = jnp.dot(modded, w_ffn, preferred_element_type=jnp.float32)
    pre = pre + jnp.dot(lowrank, adapter_feedforward_up, preferred_element_type=jnp.float32)
    activation = jax.nn.gelu(pre, approximate=True).astype(jnp.bfloat16)
    qkv = qkv.reshape(PTOK, 3, HEADS, DH)
    queries = rms_unit(qkv[:, 0]).astype(jnp.bfloat16)
    keys_new = rms_unit(qkv[:, 1]).astype(jnp.bfloat16)
    values_new = qkv[:, 2].astype(jnp.bfloat16)
    picked = jnp.take(cache, blocks, axis=0)
    cached_keys = rms_unit(picked[:, :, 0].reshape(NSEL * BLK, HEADS, DH).astype(jnp.float32)).astype(jnp.bfloat16)
    cached_values = picked[:, :, 1].reshape(NSEL * BLK, HEADS, DH)
    all_keys = jnp.concatenate([keys_new, cached_keys], axis=0).astype(jnp.float32)
    all_values = jnp.concatenate([values_new, cached_values], axis=0).astype(jnp.float32)
    scores = jnp.einsum('qhd,khd->hqk', queries.astype(jnp.float32), all_keys) / math.sqrt(DH)
    expo = jnp.exp(scores)
    weights = (expo / lax.optimization_barrier(jnp.sum(expo, axis=-1, keepdims=True))).astype(jnp.bfloat16)
    mixed = jnp.einsum('hqk,khd->qhd', weights.astype(jnp.float32), all_values).astype(jnp.bfloat16)
    mixed = mixed.reshape(PTOK, N_HEAD, ATTENTION_WIDTH // N_HEAD).astype(jnp.float32)
    grouped = activation.reshape(PTOK, N_HEAD, FEEDFWD_HIDDEN // N_HEAD).astype(jnp.float32)
    rows_attn = out_attn.reshape(N_HEAD, ATTENTION_WIDTH // N_HEAD, MODEL_WIDTH).astype(jnp.float32)
    rows_ffn = out_ffn.reshape(N_HEAD, FEEDFWD_HIDDEN // N_HEAD, MODEL_WIDTH).astype(jnp.float32)
    partial_value = jnp.einsum('qgc,gcd->gqd', mixed, rows_attn) + jnp.einsum('qgf,gfd->gqd', grouped, rows_ffn)
    rounded = lax.optimization_barrier(partial_value.astype(jnp.bfloat16))
    branch = lax.optimization_barrier(jnp.sum(rounded.astype(jnp.float32), axis=0))
    return (resid.astype(jnp.float32) + gate * branch).astype(jnp.bfloat16)

def reference(latents, patch_numbers, prior_step_cache, old_block_index, modulation_offset, modulation_scale, modulation_gate, query_key_value_weight, feedforward_input_weight, adapter_down_weight, adapter_up_query_key_value, adapter_up_feedforward, attention_output_weight, feedforward_output_weight):
    layers_out = []
    current_rows = [latents[patch_numbers[layer_index]] for layer_index in range(PATCHES)]
    for layer_step in range(LAYER_COUNT):
        row = []
        for layer_index in range(PATCHES):
            layer_output = single_layer_body(current_rows[layer_index], old_block_index[layer_step, layer_index], prior_step_cache[layer_step], modulation_offset[layer_step], modulation_scale[layer_step], modulation_gate[layer_step], query_key_value_weight[layer_step], feedforward_input_weight[layer_step], adapter_down_weight[layer_step], adapter_up_query_key_value[layer_step], adapter_up_feedforward[layer_step], attention_output_weight[layer_step], feedforward_output_weight[layer_step])
            row.append(layer_output)
        current_rows = row
        layers_out.append(jnp.stack(row, axis=0))
    return jnp.stack(layers_out, axis=0)
```

```python
import math

import jax
import jax.numpy as jnp
from jax import lax
from jax.experimental import pallas as pl
from jax.experimental.pallas import tpu as pltpu
from jax.sharding import PartitionSpec as P

DH = 128
MESH = pl.DeviceIdType.MESH
F32 = jnp.float32
BF16 = jnp.bfloat16
A, B = 0, 1

XP, XM, YP, YM = (1, 0), (-1, 0), (0, 1), (0, -1)
GATHER = [
    (-1, None, None, (0, 0), XP),
    (-1, None, None, (0, 0), XM),
    (-1, None, None, (0, 0), YP),
    (-1, None, None, (0, 0), YM),
    (0, 0, None, XM, XP),
    (0, None, A, XM, YP),
    (0, None, A, XM, YM),
    (1, 1, None, XP, XM),
    (1, None, A, XP, YP),
    (1, None, A, XP, YM),
    (2, 0, None, YM, YP),
    (2, None, B, YM, XP),
    (2, None, B, YM, XM),
    (3, 1, None, YP, YM),
    (3, None, B, YP, XP),
    (3, None, B, YP, XM),
    (4, 0, A, (2, 0), YP),
    (4, 0, A, (2, 0), YM),
    (7, 1, A, (2, 0), YP),
    (7, 1, A, (2, 0), YM),
    (10, 0, B, (0, 2), XP),
    (10, 0, B, (0, 2), XM),
    (13, 1, B, (0, 2), XP),
    (13, 1, B, (0, 2), XM),
    (5, 0, A, (-1, -1), YP),
    (6, 1, A, (-1, 1), YM),
    (8, 0, A, (1, -1), YP),
    (9, 1, A, (1, 1), YM),
    (11, 0, B, (-1, -1), XP),
    (12, 1, B, (1, -1), XM),
    (14, 0, B, (-1, 1), XP),
    (15, 1, B, (1, 1), XM),
    (16, 0, A, (2, -1), YP),
    (19, 1, A, (2, 1), YM),
    (20, 0, B, (-1, 2), XP),
    (23, 1, B, (1, 2), XM),
]
GATHER_WAITS = [0, 1, 2, 3, 4, 7, 10, 13, 5, 6, 8, 9, 11, 12, 14, 15, 16, 19, 20, 23]


def rms_unit(values):
    return values * lax.rsqrt(jnp.mean(values * values, axis=-1, keepdims=True) + 1e-06)


def kernel(
    lat, pn, bidx, off, scl, gate, upq, upf, dnt, cache_hbm, wqkv_hbm, wffn_hbm, woa_hbm, wof_hbm,
    out,
    win, wout, cachev, skv, r1, kv, xin, xg, act, part, rb, tb, r2,
    ag_s, ag_r, rs_s, rs_r, st_s, st_r, x_s, x_r, w_sem,
):
    patches = xin.shape[0]
    sections = lax.axis_size("section")
    sec = lax.axis_index("section")
    head = lax.axis_index("head")
    x = head // 4
    y = lax.rem(head, 4)

    def px(d):
        return lax.rem(x + (d + 4), 4)

    def py(d):
        return lax.rem(y + (d + 4), 4)

    def dev(d):
        return (sec, px(d[0]) * 4 + py(d[1]))

    first_section = sec == 0
    last_section = sec == sections - 1

    w_copies = [
        pltpu.make_async_copy(cache_hbm, cachev, w_sem.at[0]),
        pltpu.make_async_copy(wqkv_hbm.at[0], win.at[:, pl.ds(0, DH)], w_sem.at[1]),
        pltpu.make_async_copy(wqkv_hbm.at[1], win.at[:, pl.ds(DH, DH)], w_sem.at[2]),
        pltpu.make_async_copy(wqkv_hbm.at[2], win.at[:, pl.ds(2 * DH, DH)], w_sem.at[3]),
        pltpu.make_async_copy(wffn_hbm, win.at[:, pl.ds(3 * DH, 768)], w_sem.at[4]),
        pltpu.make_async_copy(woa_hbm, wout.at[pl.ds(0, DH)], w_sem.at[5]),
        pltpu.make_async_copy(wof_hbm, wout.at[pl.ds(DH, 768)], w_sem.at[6]),
    ]
    for copy in w_copies:
        copy.start()

    barrier = pltpu.get_barrier_semaphore()
    for d in (XP, XM, (2, 0), YP, YM, (0, 2)):
        pl.semaphore_signal(barrier, inc=1, device_id=dev(d), device_id_type=MESH)

    for step in (1, sections - 1):
        neighbour = (lax.rem(sec + step, sections), head)
        pl.semaphore_signal(barrier, inc=1, device_id=neighbour, device_id_type=MESH)
    pl.semaphore_wait(barrier, 8)

    def remote(src, dst, ssem, rsem, device):
        return pltpu.make_async_remote_copy(
            src_ref=src, dst_ref=dst, send_sem=ssem, recv_sem=rsem, device_id=device,
            device_id_type=MESH,
        )

    def xg_at(m, q, hf, place):
        qi = slice(None) if q is None else q
        hi = slice(None) if hf is None else hf
        return xg.at[m, qi, hi, px(place[0]), py(place[1])]

    def gather_copy(m, i):
        _, q, hf, place, way = GATHER[i]
        ref = xg_at(m, q, hf, place)
        return remote(ref, ref, ag_s.at[m, i], ag_r.at[m, i], dev(way))

    def gather_landed(m, i):
        _, q, hf, place, way = GATHER[i]
        ref = xg_at(m, q, hf, (place[0] - way[0], place[1] - way[1]))
        remote(ref, ref, ag_s.at[m, i], ag_r.at[m, i], dev((-way[0], -way[1]))).wait_recv()

    def stale_first(m, i):
        if i < 3:
            d = (1, -1, 2)[i]
            return remote(
                skv.at[m, 0, px(d)], r1.at[m, 0, x], st_s.at[m, i], st_r.at[m, i], dev((d, 0))
            )
        d = (1, -1, 2)[i - 3]
        return remote(
            skv.at[m, 1, py(d)], r1.at[m, 1, y], st_s.at[m, i], st_r.at[m, i], dev((0, d))
        )

    def stale_first_landed(m, i):
        if i < 3:
            d = (-1, 1, 2)[i]
            ref, device = r1.at[m, 0, px(d)], dev((d, 0))
        else:
            d = (-1, 1, 2)[i - 3]
            ref, device = r1.at[m, 1, py(d)], dev((0, d))
        remote(ref, ref, st_s.at[m, i], st_r.at[m, i], device).wait_recv()

    def stale_second(m, i):
        if i < 9:
            d = (1, -1, 2)[i - 6]
            return remote(
                r1.at[m, 0, :, py(d)], kv.at[m, 0, y], st_s.at[m, i], st_r.at[m, i], dev((0, d))
            )
        d = (1, -1, 2)[i - 9]
        return remote(
            r1.at[m, 1, :, px(d)], kv.at[m, 1, x], st_s.at[m, i], st_r.at[m, i], dev((d, 0))
        )

    def stale_second_landed(m, i):
        if i < 9:
            d = (-1, 1, 2)[i - 6]
            ref, device = kv.at[m, 0, py(d)], dev((0, d))
        else:
            d = (-1, 1, 2)[i - 9]
            ref, device = kv.at[m, 1, px(d)], dev((d, 0))
        remote(ref, ref, st_s.at[m, i], st_r.at[m, i], device).wait_recv()

    def stale_send(m):
        def one(j, _):
            block = bidx[m, j]
            keys = cachev[0, block].astype(F32)
            values = cachev[1, block]
            rows = pl.ds(pl.multiple_of(j * 16, 16), 16)
            for h in range(16):
                part_k = keys[:, h * DH:(h + 1) * DH]
                skv[m, 0, h // 4, h % 4, rows, :] = rms_unit(part_k).astype(BF16)
                skv[m, 1, h % 4, h // 4, rows, :] = values[:, h * DH:(h + 1) * DH]
            return 0

        lax.fori_loop(0, 4, one, 0)
        for i in range(6):
            stale_first(m, i).start()
        r1[m, 0, x] = skv[m, 0, x]
        r1[m, 1, y] = skv[m, 1, y]

    def stale_forward(m):
        for i in range(3):
            stale_first_landed(m, i)
        for i in range(6, 9):
            stale_second(m, i).start()
        for i in range(3, 6):
            stale_first_landed(m, i)
        for i in range(9, 12):
            stale_second(m, i).start()
        kv[m, 0, y] = r1[m, 0, :, y]
        kv[m, 1, x] = r1[m, 1, :, x]

    ALL = slice(None)
    SUM1 = [
        (lambda m: part.at[m, 0, A, :, py(2)], YM),
        (lambda m: part.at[m, 0, A, :, py(1)], YP),
        (lambda m: part.at[m, 0, B, px(2)], XM),
        (lambda m: part.at[m, 0, B, px(1)], XP),
        (lambda m: part.at[m, 1, A, :, py(2)], YP),
        (lambda m: part.at[m, 1, A, :, py(-1)], YM),
        (lambda m: part.at[m, 1, B, px(2)], XP),
        (lambda m: part.at[m, 1, B, px(-1)], XM),
        (lambda m: part.at[m, 0, A, :, py(-1)], YM),
        (lambda m: part.at[m, 0, B, px(-1)], XM),
        (lambda m: part.at[m, 1, A, :, py(1)], YP),
        (lambda m: part.at[m, 1, B, px(1)], XP),
    ]
    SUM2 = [
        (lambda m: tb.at[m, 0, A, px(2)], XM),
        (lambda m: tb.at[m, 0, A, px(1)], XP),
        (lambda m: tb.at[m, 0, B, py(2)], YM),
        (lambda m: tb.at[m, 0, B, py(1)], YP),
        (lambda m: tb.at[m, 1, A, px(2)], XP),
        (lambda m: tb.at[m, 1, A, px(-1)], XM),
        (lambda m: tb.at[m, 1, B, py(2)], YP),
        (lambda m: tb.at[m, 1, B, py(-1)], YM),
        (lambda m: tb.at[m, 0, A, px(-1)], XM),
        (lambda m: tb.at[m, 0, B, py(-1)], YM),
        (lambda m: tb.at[m, 1, A, px(1)], XP),
        (lambda m: tb.at[m, 1, B, py(1)], YP),
    ]

    def sum_copy(m, i):
        source, way = SUM1[i] if i < 12 else SUM2[i - 12]
        target = rb.at[m, i] if i < 12 else r2.at[m, i - 12]
        return remote(source(m), target, rs_s.at[m, i], rs_r.at[m, i], dev(way))

    def sum_landed(m, i):
        way = SUM1[i][1] if i < 12 else SUM2[i - 12][1]
        target = rb.at[m, i] if i < 12 else r2.at[m, i - 12]
        remote(
            target, target, rs_s.at[m, i], rs_r.at[m, i], dev((-way[0], -way[1]))
        ).wait_recv()

    def hand_on(m):
        return remote(out.at[m], xin.at[m], x_s.at[m], x_r.at[m], (sec + 1, head))

    def modulate_and_send(m):
        @pl.when(first_section)
        def _():
            xin[m] = lat[pn[m]]

        @pl.when(sec > 0)
        def _():
            remote(xin.at[m], xin.at[m], x_s.at[m], x_r.at[m], (sec - 1, head)).wait_recv()

        values = xin[m].astype(F32)
        center = values - jnp.mean(values, axis=-1, keepdims=True)
        spread = jnp.mean(center * center, axis=-1, keepdims=True)
        normed = center * lax.rsqrt(spread + 1e-06)
        modded = (normed * (1.0 + scl[...]) + off[...]).astype(BF16)
        for q in range(2):
            for hf in range(2):
                c = q * 2 + hf
                xg[m, q, hf, x, y] = modded[:, c * 768:(c + 1) * 768]
        for i in range(4):
            gather_copy(m, i).start()

    def gather_rest(m):
        for w in GATHER_WAITS:
            gather_landed(m, w)
            for i, entry in enumerate(GATHER):
                if entry[0] == w:
                    gather_copy(m, i).start()
        for i in range(len(GATHER)):
            if i not in GATHER_WAITS:
                gather_landed(m, i)

    def tokens(m, c):
        return xg[m, c // 2, c % 2].reshape(256, 768)

    def dot(a, b):
        return jnp.dot(a, b, preferred_element_type=F32)

    def dot_nt(a, b):
        return lax.dot_general(a, b, (((1,), (1,)), ((), ())), preferred_element_type=F32)

    def project(m):
        low = dot_nt(tokens(m, 0), dnt[:, 0:768])
        for c in range(1, 4):
            low += dot_nt(tokens(m, c), dnt[:, c * 768:(c + 1) * 768])
        low = low.astype(BF16)
        qkv = []
        for n in range(3):
            acc = dot(low, upq[n])
            for c in range(4):
                acc += dot(tokens(m, c), win[c * 768:(c + 1) * 768, n * DH:(n + 1) * DH])
            qkv.append(acc)

        def feed(n, _):
            cols = pl.ds(pl.multiple_of(n * 256, 256), 256)
            wcols = pl.ds(pl.multiple_of(n * 256 + 3 * DH, DH), 256)
            acols = pl.ds(pl.multiple_of(n * 256 + DH, DH), 256)
            acc = dot(low, upf[:, cols])
            for c in range(4):
                acc += dot(tokens(m, c), win[c * 768:(c + 1) * 768, wcols])
            act[:, acols] = jax.nn.gelu(acc, approximate=True).astype(BF16)
            return 0

        lax.fori_loop(0, 3, feed, 0)
        return qkv

    def attend(m, qkv):
        queries = rms_unit(qkv[0]).astype(BF16)
        fresh_keys = rms_unit(qkv[1]).astype(BF16)
        fresh_values = qkv[2].astype(BF16)
        for i in range(6, 12):
            stale_second_landed(m, i)
        total = jnp.zeros((256, 1), F32)
        mixed = jnp.zeros((256, DH), F32)
        for j in range(5):
            if j == 4:
                keys, values = fresh_keys, fresh_values
            else:
                keys = kv[m, 0, j].reshape(256, DH)
                values = kv[m, 1, :, j].reshape(256, DH)
            expo = jnp.exp(dot_nt(queries, keys) * (1.0 / math.sqrt(DH)))
            total += jnp.sum(expo, axis=-1, keepdims=True)
            mixed += dot(expo.astype(BF16), values)
        act[:, 0:DH] = (mixed / total).astype(BF16)

    def output_products(m):
        for q in range(2):
            for hf in range(2):
                c = q * 2 + hf
                for n in range(3):
                    lo = c * 768 + n * 256
                    term = dot(act[...], wout[:, lo:lo + 256]).astype(BF16)
                    part[m, q, hf, :, :, :, n * 256:(n + 1) * 256] = term.reshape(4, 4, 16, 256)
                sum_copy(m, 2 * c).start()
                sum_copy(m, 2 * c + 1).start()

    def wide(value):
        return value.astype(F32)

    def sum_up(m):
        sum_landed(m, 0)
        part[m, 0, A, :, py(-1)] = (wide(part[m, 0, A, :, py(-1)]) + wide(rb[m, 0])).astype(BF16)
        sum_copy(m, 8).start()
        sum_landed(m, 2)
        part[m, 0, B, px(-1)] = (wide(part[m, 0, B, px(-1)]) + wide(rb[m, 2])).astype(BF16)
        sum_copy(m, 9).start()
        sum_landed(m, 4)
        part[m, 1, A, :, py(1)] = (wide(part[m, 1, A, :, py(1)]) + wide(rb[m, 4])).astype(BF16)
        sum_copy(m, 10).start()
        sum_landed(m, 6)
        part[m, 1, B, px(1)] = (wide(part[m, 1, B, px(1)]) + wide(rb[m, 6])).astype(BF16)
        sum_copy(m, 11).start()
        for q, hf, near, far, a, b in (
            (0, A, 1, 8, 12, 13), (0, B, 3, 9, 14, 15), (1, A, 5, 10, 16, 17), (1, B, 7, 11, 18, 19)
        ):
            sum_landed(m, near)
            sum_landed(m, far)
            mine = part[m, q, hf, :, y] if hf == A else part[m, q, hf, x]
            tb[m, q, hf] = (wide(mine) + wide(rb[m, near]) + wide(rb[m, far])).astype(BF16)
            sum_copy(m, a).start()
            sum_copy(m, b).start()
        for q, hf, came, i in ((0, A, 12, 20), (0, B, 14, 21), (1, A, 16, 22), (1, B, 18, 23)):
            step = -1 if q == 0 else 1
            place = px(step) if hf == A else py(step)
            sum_landed(m, came)
            tb[m, q, hf, place] = (wide(tb[m, q, hf, place]) + wide(r2[m, came - 12])).astype(BF16)
            sum_copy(m, i).start()
        for q, hf, near, far, n1, n2 in (
            (0, A, 1, 8, 13, 20), (0, B, 3, 9, 15, 21), (1, A, 5, 10, 17, 22), (1, B, 7, 11, 19, 23)
        ):
            sum_landed(m, n1)
            sum_landed(m, n2)
            along = x if hf == A else y
            branch = wide(part[m, q, hf, x, y]) + wide(rb[m, near, along]) + wide(rb[m, far, along])
            branch += wide(r2[m, n1 - 12]) + wide(r2[m, n2 - 12])
            c = q * 2 + hf
            cols = slice(c * 768, (c + 1) * 768)
            out[m, :, cols] = (wide(xin[m, :, cols]) + gate[:, cols] * branch).astype(BF16)

        @pl.when(sec < sections - 1)
        def _():
            hand_on(m).start()

    w_copies[0].wait()
    stale_send(0)

    def patch(m, _):
        modulate_and_send(m)

        @pl.when(m == 0)
        def _():
            stale_forward(0)

        gather_rest(m)

        @pl.when(m == 0)
        def _():
            for copy in w_copies[1:]:
                copy.wait()

        @pl.when(m < patches - 1)
        def _():
            stale_send(m + 1)

        attend(m, project(m))
        output_products(m)

        @pl.when(m < patches - 1)
        def _():
            stale_forward(m + 1)

        sum_up(m)
        return 0

    lax.fori_loop(0, patches, patch, 0)

    def drain(m, _):
        for i in range(len(GATHER)):
            gather_copy(m, i).wait_send()
        for i in range(24):
            sum_copy(m, i).wait_send()
        for i in range(6):
            stale_first(m, i).wait_send()
        for i in range(6, 12):
            stale_second(m, i).wait_send()

        @pl.when(sec < sections - 1)
        def _():
            hand_on(m).wait_send()

        return 0

    lax.fori_loop(0, patches, drain, 0)


def per_device(
    latents, patch_numbers, prior_step_cache, old_block_index, modulation_offset, modulation_scale,
    modulation_gate, query_key_value_weight, feedforward_input_weight, adapter_down_weight,
    adapter_up_query_key_value, adapter_up_feedforward, attention_output_weight,
    feedforward_output_weight,
):
    patches = old_block_index.shape[1]
    vmem = pl.BlockSpec(memory_space=pltpu.VMEM)
    smem = pl.BlockSpec(memory_space=pltpu.SMEM)
    hbm = pl.BlockSpec(memory_space=pl.ANY)
    dma = pltpu.SemaphoreType.DMA
    record = pl.pallas_call(
        kernel,
        out_shape=jax.ShapeDtypeStruct((patches, 16, 3072), BF16),
        in_specs=[vmem, smem, smem] + [vmem] * 6 + [hbm] * 5,
        out_specs=vmem,
        scratch_shapes=[
            pltpu.VMEM((3072, 1152), BF16),
            pltpu.VMEM((896, 3072), BF16),
            pltpu.VMEM((2, 16, 16, 2048), BF16),
            pltpu.VMEM((patches, 2, 4, 4, 64, DH), BF16),
            pltpu.VMEM((patches, 2, 4, 4, 64, DH), BF16),
            pltpu.VMEM((patches, 2, 4, 4, 64, DH), BF16),
            pltpu.VMEM((patches, 16, 3072), BF16),
            pltpu.VMEM((patches, 2, 2, 4, 4, 16, 768), BF16),
            pltpu.VMEM((256, 896), BF16),
            pltpu.VMEM((patches, 2, 2, 4, 4, 16, 768), BF16),
            pltpu.VMEM((patches, 12, 4, 16, 768), BF16),
            pltpu.VMEM((patches, 2, 2, 4, 16, 768), BF16),
            pltpu.VMEM((patches, 12, 16, 768), BF16),
            dma((patches, 36)),
            dma((patches, 36)),
            dma((patches, 24)),
            dma((patches, 24)),
            dma((patches, 12)),
            dma((patches, 12)),
            dma((patches,)),
            dma((patches,)),
            dma((7,)),
        ],
        compiler_params=pltpu.CompilerParams(
            collective_id=0, has_side_effects=True, vmem_limit_bytes=58 * 2**20
        ),
        cost_estimate=pl.CostEstimate(
            flops=10_000_000_000, bytes_accessed=16_000_000, transcendentals=2_000_000
        ),
    )(
        latents,
        patch_numbers,
        old_block_index[0],
        modulation_offset,
        modulation_scale,
        modulation_gate,
        adapter_up_query_key_value[0].transpose(1, 0, 2),
        adapter_up_feedforward[0],
        adapter_down_weight[0].T,
        prior_step_cache[0].transpose(2, 0, 1, 3),
        query_key_value_weight[0].transpose(1, 0, 2),
        feedforward_input_weight[0],
        attention_output_weight[0],
        feedforward_output_weight[0],
    )
    return record[None]


def solution(mesh):
    placed = (
        P(None, "head", None),
        P(),
        P("section", None, "head", None, None),
        P("section", None, None),
        P("section", None),
        P("section", None),
        P("section", None),
        P("section", None, None, "head"),
        P("section", None, "head"),
        P("section", None, None),
        P("section", None, None, "head"),
        P("section", None, "head"),
        P("section", "head", None),
        P("section", "head", None),
    )
    return jax.shard_map(
        per_device,
        mesh=mesh,
        in_specs=placed,
        out_specs=P("section", None, "head", None),
        check_vma=False,
    )
```

```python
import math

import jax
import jax.numpy as jnp
from jax import lax
from jax.experimental import pallas as pl
from jax.experimental.pallas import tpu as pltpu
from jax.sharding import PartitionSpec as P

DH = 128
MESH = pl.DeviceIdType.MESH
F32 = jnp.float32
BF16 = jnp.bfloat16
A, B = 0, 1

ORDER = [
    (0, 0), (1, 0), (3, 0), (2, 0), (0, 1), (0, 3), (0, 2),
    (1, 1), (1, 3), (3, 1), (3, 3), (1, 2), (3, 2), (2, 1), (2, 3), (2, 2),
]
EARLY = 7 * 16
FAR_FIRST = (2, 1, 3)
NEAR_FIRST = (1, 3, 2)


def along(axis, d):
    return (d, 0) if axis == 0 else (0, d)


def slot(place):
    return ORDER.index((place[0] % 4, place[1] % 4))


GATHER = []
for axis in (0, 1):
    GATHER += [(axis, (0, 0), along(axis, d)) for d in FAR_FIRST]
for axis in (0, 1):
    GATHER += [(1 - axis, (0, 0), along(axis, d)) for d in FAR_FIRST]
FORWARD = []
for d in NEAR_FIRST:
    for axis in (0, 1):
        first = GATHER.index((axis, (0, 0), along(axis, d)))
        after = [(axis, along(axis, -d % 4), along(1 - axis, e)) for e in FAR_FIRST]
        FORWARD.append((first, range(len(GATHER), len(GATHER) + 3)))
        GATHER += after


def rms_unit(values):
    return values * lax.rsqrt(jnp.mean(values * values, axis=-1, keepdims=True) + 1e-06)


def kernel(
    lat, pn, bidx, off, scl, gate, upq, upf, dnt, cache_hbm, wqkv_hbm, wffn_hbm, woa_hbm, wof_hbm,
    out,
    win, wout, cachev, skv, r1, kv, xin, xg, qkv, act, part, rb, tb, r2,
    ag_s, ag_r, rs_s, rs_r, st_s, st_r, x_s, x_r, w_sem,
):
    patches = xin.shape[0]
    sections = lax.axis_size("section")
    sec = lax.axis_index("section")
    head = lax.axis_index("head")
    x = head // 4
    y = lax.rem(head, 4)

    def px(d):
        return lax.rem(x + (d + 4), 4)

    def py(d):
        return lax.rem(y + (d + 4), 4)

    def dev(d):
        return (sec, px(d[0]) * 4 + py(d[1]))

    first_section = sec == 0
    last_section = sec == sections - 1

    w_copies = [
        pltpu.make_async_copy(cache_hbm, cachev, w_sem.at[0]),
        pltpu.make_async_copy(wqkv_hbm.at[0], win.at[:, pl.ds(0, DH)], w_sem.at[1]),
        pltpu.make_async_copy(wqkv_hbm.at[1], win.at[:, pl.ds(DH, DH)], w_sem.at[2]),
        pltpu.make_async_copy(wqkv_hbm.at[2], win.at[:, pl.ds(2 * DH, DH)], w_sem.at[3]),
        pltpu.make_async_copy(wffn_hbm, win.at[:, pl.ds(3 * DH, 768)], w_sem.at[4]),
        pltpu.make_async_copy(woa_hbm, wout.at[pl.ds(0, DH)], w_sem.at[5]),
        pltpu.make_async_copy(wof_hbm, wout.at[pl.ds(DH, 768)], w_sem.at[6]),
    ]
    for copy in w_copies:
        copy.start()

    barrier = pltpu.get_barrier_semaphore()
    for d in FAR_FIRST:
        for axis in (0, 1):
            pl.semaphore_signal(
                barrier, inc=1, device_id=dev(along(axis, d)), device_id_type=MESH
            )
    for step in (1, sections - 1):
        neighbour = (lax.rem(sec + step, sections), head)
        pl.semaphore_signal(barrier, inc=1, device_id=neighbour, device_id_type=MESH)
    pl.semaphore_wait(barrier, 8)

    def remote(src, dst, ssem, rsem, device):
        return pltpu.make_async_remote_copy(
            src_ref=src, dst_ref=dst, send_sem=ssem, recv_sem=rsem, device_id=device,
            device_id_type=MESH,
        )

    def gather_copy(m, i):
        hf, place, way = GATHER[i]
        there = slot((place[0] - way[0], place[1] - way[1]))
        return remote(
            xg.at[m, hf, slot(place)], xg.at[m, hf, there], ag_s.at[m, i], ag_r.at[m, i], dev(way)
        )

    def gather_landed(m, i):
        hf, place, way = GATHER[i]
        ref = xg.at[m, hf, slot((place[0] - way[0], place[1] - way[1]))]
        remote(ref, ref, ag_s.at[m, i], ag_r.at[m, i], dev((-way[0], -way[1]))).wait_recv()

    def stale_first(m, i):
        if i < 3:
            d = (1, -1, 2)[i]
            return remote(
                skv.at[m, 0, px(d)], r1.at[m, 0, x], st_s.at[m, i], st_r.at[m, i], dev((d, 0))
            )
        d = (1, -1, 2)[i - 3]
        return remote(
            skv.at[m, 1, py(d)], r1.at[m, 1, y], st_s.at[m, i], st_r.at[m, i], dev((0, d))
        )

    def stale_first_landed(m, i):
        if i < 3:
            d = (-1, 1, 2)[i]
            ref, device = r1.at[m, 0, px(d)], dev((d, 0))
        else:
            d = (-1, 1, 2)[i - 3]
            ref, device = r1.at[m, 1, py(d)], dev((0, d))
        remote(ref, ref, st_s.at[m, i], st_r.at[m, i], device).wait_recv()

    def stale_second(m, i):
        if i < 9:
            d = (1, -1, 2)[i - 6]
            return remote(
                r1.at[m, 0, :, py(d)], kv.at[m, 0, y], st_s.at[m, i], st_r.at[m, i], dev((0, d))
            )
        d = (1, -1, 2)[i - 9]
        return remote(
            r1.at[m, 1, :, px(d)], kv.at[m, 1, x], st_s.at[m, i], st_r.at[m, i], dev((d, 0))
        )

    def stale_second_landed(m, i):
        if i < 9:
            d = (-1, 1, 2)[i - 6]
            ref, device = kv.at[m, 0, py(d)], dev((0, d))
        else:
            d = (-1, 1, 2)[i - 9]
            ref, device = kv.at[m, 1, px(d)], dev((d, 0))
        remote(ref, ref, st_s.at[m, i], st_r.at[m, i], device).wait_recv()

    def stale_send(m):
        def one(j, _):
            block = bidx[m, j]
            keys = cachev[0, block].astype(F32)
            values = cachev[1, block]
            rows = pl.ds(pl.multiple_of(j * 16, 16), 16)
            for h in range(16):
                part_k = keys[:, h * DH:(h + 1) * DH]
                skv[m, 0, h // 4, h % 4, rows, :] = rms_unit(part_k).astype(BF16)
                skv[m, 1, h % 4, h // 4, rows, :] = values[:, h * DH:(h + 1) * DH]
            return 0

        lax.fori_loop(0, 4, one, 0)
        for i in range(6):
            stale_first(m, i).start()
        r1[m, 0, x] = skv[m, 0, x]
        r1[m, 1, y] = skv[m, 1, y]

    def stale_forward(m):
        for i in range(3):
            stale_first_landed(m, i)
        for i in range(6, 9):
            stale_second(m, i).start()
        for i in range(3, 6):
            stale_first_landed(m, i)
        for i in range(9, 12):
            stale_second(m, i).start()
        kv[m, 0, y] = r1[m, 0, :, y]
        kv[m, 1, x] = r1[m, 1, :, x]

    def sum_way(i):
        second, c, d = i // 12, i % 12 // 3, FAR_FIRST[i % 3]
        return c, d, along((1 - c % 2) if second == 0 else c % 2, d)

    def sum_copy(m, i):
        c, d, way = sum_way(i)
        if i < 12:
            source = part.at[m, c, :, d] if c % 2 == 0 else part.at[m, c, d]
            target = rb.at[m, i]
        else:
            source, target = tb.at[m, c, d], r2.at[m, i - 12]
        return remote(source, target, rs_s.at[m, i], rs_r.at[m, i], dev(way))

    def sum_landed(m, i):
        _, _, way = sum_way(i)
        target = rb.at[m, i] if i < 12 else r2.at[m, i - 12]
        remote(
            target, target, rs_s.at[m, i], rs_r.at[m, i], dev((-way[0], -way[1]))
        ).wait_recv()

    def hand_on(m):
        return remote(out.at[m], xin.at[m], x_s.at[m], x_r.at[m], (sec + 1, head))

    def modulate_and_send(m):
        @pl.when(first_section)
        def _():
            xin[m] = lat[pn[m]]

        @pl.when(sec > 0)
        def _():
            remote(xin.at[m], xin.at[m], x_s.at[m], x_r.at[m], (sec - 1, head)).wait_recv()

        values = xin[m].astype(F32)
        center = values - jnp.mean(values, axis=-1, keepdims=True)
        spread = jnp.mean(center * center, axis=-1, keepdims=True)
        normed = center * lax.rsqrt(spread + 1e-06)
        modded = (normed * (1.0 + scl[...]) + off[...]).astype(BF16)
        xg[m, A, 0] = modded[:, :1536]
        xg[m, B, 0] = modded[:, 1536:]
        for i in range(12):
            gather_copy(m, i).start()

    def gather_forward(m):
        for first, after in FORWARD:
            gather_landed(m, first)
            for i in after:
                gather_copy(m, i).start()
        for i in range(6, 12):
            gather_landed(m, i)

    def gather_rest(m):
        for i in range(12, len(GATHER)):
            gather_landed(m, i)

    def dot(a, b):
        return jnp.dot(a, b, preferred_element_type=F32)

    def dot_tn(a, b):
        return lax.dot_general(a, b, (((0,), (0,)), ((), ())), preferred_element_type=F32)

    def dot_nt(a, b):
        return lax.dot_general(a, b, (((1,), (1,)), ((), ())), preferred_element_type=F32)

    def merge(i, _):
        rows = pl.ds(pl.multiple_of(i * 256, 256), 256)
        down = dnt[:, rows]
        for n in range(3):
            win[rows, n * DH:(n + 1) * DH] = (
                win[rows, n * DH:(n + 1) * DH].astype(F32) + dot_tn(down, upq[n])
            ).astype(BF16)
            cols = slice(3 * DH + n * 256, 3 * DH + (n + 1) * 256)
            win[rows, cols] = (
                win[rows, cols].astype(F32) + dot_tn(down, upf[:, n * 256:(n + 1) * 256])
            ).astype(BF16)
        return 0

    def project(m, lo, hi):
        def tile(first, width):
            acc = None
            for hf in range(2):
                rows = xg[m, hf, lo // 16:hi // 16].reshape(hi - lo, 1536)
                term = dot(rows, win[hf * 1536:(hf + 1) * 1536, pl.ds(first, width)])
                acc = term if acc is None else acc + term
            return acc

        qkv[lo:hi, 0:256] = tile(0, 256)
        qkv[lo:hi, 256:384] = tile(256, DH)

        def feed(n, _):
            cols = pl.ds(pl.multiple_of(n * 256 + DH, DH), 256)
            acc = tile(pl.multiple_of(n * 256 + 3 * DH, DH), 256)
            act[lo:hi, cols] = jax.nn.gelu(acc, approximate=True).astype(BF16)
            return 0

        lax.fori_loop(0, 3, feed, 0)

    def attend(m):
        queries = rms_unit(qkv[:, 0:DH]).astype(BF16)
        fresh_keys = rms_unit(qkv[:, DH:2 * DH]).astype(BF16)
        fresh_values = qkv[:, 2 * DH:3 * DH].astype(BF16)
        for i in range(6, 12):
            stale_second_landed(m, i)
        total = jnp.zeros((256, 1), F32)
        mixed = jnp.zeros((256, DH), F32)
        for j in range(5):
            if j == 4:
                keys, values = fresh_keys, fresh_values
            else:
                keys = kv[m, 0, j].reshape(256, DH)
                values = kv[m, 1, :, j].reshape(256, DH)
            expo = jnp.exp(dot_nt(queries, keys) * (1.0 / math.sqrt(DH)))
            total += jnp.sum(expo, axis=-1, keepdims=True)
            mixed += dot(expo.astype(BF16), values)
        act[:, 0:DH] = (mixed / total).astype(BF16)

    def output_products(m):
        for c in range(4):
            for n in range(3):
                lo = c * 768 + n * 256
                term = dot(act[...], wout[:, lo:lo + 256]).astype(BF16)
                for k, place in enumerate(ORDER):
                    rows = term[k * 16:(k + 1) * 16]
                    part[m, c, place[0], place[1], :, n * 256:(n + 1) * 256] = rows
            for j in range(3):
                sum_copy(m, 3 * c + j).start()

    def wide(value):
        return value.astype(F32)

    def sum_up(m):
        for c in range(4):
            total = wide(part[m, c, :, 0] if c % 2 == 0 else part[m, c, 0])
            for j in range(3):
                sum_landed(m, 3 * c + j)
                total += wide(rb[m, 3 * c + j])
            tb[m, c] = total.astype(BF16)
            for j in range(3):
                sum_copy(m, 12 + 3 * c + j).start()
        for c in range(4):
            branch = wide(part[m, c, 0, 0])
            for j in range(3):
                branch += wide(rb[m, 3 * c + j, 0])
            for j in range(3):
                sum_landed(m, 12 + 3 * c + j)
                branch += wide(r2[m, 3 * c + j])
            cols = slice(c * 768, (c + 1) * 768)
            out[m, :, cols] = (wide(xin[m, :, cols]) + gate[:, cols] * branch).astype(BF16)

        @pl.when(sec < sections - 1)
        def _():
            hand_on(m).start()

    def stale_send_step(m, _):
        stale_send(m)
        return 0

    def stale_forward_step(m, _):
        stale_forward(m)
        return 0

    ahead = jnp.where(sec == 0, 0, jnp.where(sec == 1, 1, patches))
    w_copies[0].wait()
    lax.fori_loop(0, ahead, stale_send_step, 0)

    @pl.when(sec > 0)
    def _():
        for copy in w_copies[1:5]:
            copy.wait()

    lax.fori_loop(0, jnp.where(sec == 0, 0, 12), merge, 0)
    lax.fori_loop(0, ahead, stale_forward_step, 0)

    def patch(m, _):
        opening = jnp.logical_and(sec == 0, m == 0)
        more_stale = jnp.logical_and(sec < 2, m < patches - 1)
        modulate_and_send(m)

        @pl.when(opening)
        def _():
            stale_send(0)

        gather_forward(m)

        @pl.when(opening)
        def _():
            for copy in w_copies[1:5]:
                copy.wait()
            lax.fori_loop(0, 12, merge, 0)
            stale_forward(0)

        project(m, 0, EARLY)
        gather_rest(m)
        project(m, EARLY, 256)

        @pl.when(more_stale)
        def _():
            stale_send(m + 1)

        attend(m)

        @pl.when(m == 0)
        def _():
            for copy in w_copies[5:]:
                copy.wait()

        output_products(m)

        @pl.when(more_stale)
        def _():
            stale_forward(m + 1)

        sum_up(m)
        return 0

    lax.fori_loop(0, patches, patch, 0)

    def drain(m, _):
        for i in range(len(GATHER)):
            gather_copy(m, i).wait_send()
        for i in range(24):
            sum_copy(m, i).wait_send()
        for i in range(6):
            stale_first(m, i).wait_send()
        for i in range(6, 12):
            stale_second(m, i).wait_send()

        @pl.when(sec < sections - 1)
        def _():
            hand_on(m).wait_send()

        return 0

    lax.fori_loop(0, patches, drain, 0)


def per_device(
    latents, patch_numbers, prior_step_cache, old_block_index, modulation_offset, modulation_scale,
    modulation_gate, query_key_value_weight, feedforward_input_weight, adapter_down_weight,
    adapter_up_query_key_value, adapter_up_feedforward, attention_output_weight,
    feedforward_output_weight,
):
    patches = old_block_index.shape[1]
    vmem = pl.BlockSpec(memory_space=pltpu.VMEM)
    smem = pl.BlockSpec(memory_space=pltpu.SMEM)
    hbm = pl.BlockSpec(memory_space=pl.ANY)
    dma = pltpu.SemaphoreType.DMA
    record = pl.pallas_call(
        kernel,
        out_shape=jax.ShapeDtypeStruct((patches, 16, 3072), BF16),
        in_specs=[vmem, smem, smem] + [vmem] * 6 + [hbm] * 5,
        out_specs=vmem,
        scratch_shapes=[
            pltpu.VMEM((3072, 1152), BF16),
            pltpu.VMEM((896, 3072), BF16),
            pltpu.VMEM((2, 16, 16, 2048), BF16),
            pltpu.VMEM((patches, 2, 4, 4, 64, DH), BF16),
            pltpu.VMEM((patches, 2, 4, 4, 64, DH), BF16),
            pltpu.VMEM((patches, 2, 4, 4, 64, DH), BF16),
            pltpu.VMEM((patches, 16, 3072), BF16),
            pltpu.VMEM((patches, 2, 16, 16, 1536), BF16),
            pltpu.VMEM((256, 3 * DH), F32),
            pltpu.VMEM((256, 896), BF16),
            pltpu.VMEM((patches, 4, 4, 4, 16, 768), BF16),
            pltpu.VMEM((patches, 12, 4, 16, 768), BF16),
            pltpu.VMEM((patches, 4, 4, 16, 768), BF16),
            pltpu.VMEM((patches, 12, 16, 768), BF16),
            dma((patches, len(GATHER))),
            dma((patches, len(GATHER))),
            dma((patches, 24)),
            dma((patches, 24)),
            dma((patches, 12)),
            dma((patches, 12)),
            dma((patches,)),
            dma((patches,)),
            dma((7,)),
        ],
        compiler_params=pltpu.CompilerParams(
            collective_id=0, has_side_effects=True, vmem_limit_bytes=58 * 2**20
        ),
        cost_estimate=pl.CostEstimate(
            flops=10_000_000_000, bytes_accessed=16_000_000, transcendentals=2_000_000
        ),
    )(
        latents,
        patch_numbers,
        old_block_index[0],
        modulation_offset,
        modulation_scale,
        modulation_gate,
        adapter_up_query_key_value[0].transpose(1, 0, 2),
        adapter_up_feedforward[0],
        adapter_down_weight[0].T,
        prior_step_cache[0].transpose(2, 0, 1, 3),
        query_key_value_weight[0].transpose(1, 0, 2),
        feedforward_input_weight[0],
        attention_output_weight[0],
        feedforward_output_weight[0],
    )
    return record[None]


def solution(mesh):
    placed = (
        P(None, "head", None),
        P(),
        P("section", None, "head", None, None),
        P("section", None, None),
        P("section", None),
        P("section", None),
        P("section", None),
        P("section", None, None, "head"),
        P("section", None, "head"),
        P("section", None, None),
        P("section", None, None, "head"),
        P("section", None, "head"),
        P("section", "head", None),
        P("section", "head", None),
    )
    return jax.shard_map(
        per_device,
        mesh=mesh,
        in_specs=placed,
        out_specs=P("section", None, "head", None),
        check_vma=False,
    )
```

```python
import math

import jax
import jax.numpy as jnp
from jax import lax
from jax.experimental import pallas as pl
from jax.experimental.pallas import tpu as pltpu
from jax.sharding import PartitionSpec as P

DH = 128
MESH = pl.DeviceIdType.MESH
F32 = jnp.float32
BF16 = jnp.bfloat16
A, B = 0, 1

ORDER = [
    (0, 0), (1, 0), (3, 0), (2, 0), (0, 1), (0, 3), (0, 2),
    (1, 1), (1, 3), (3, 1), (3, 3), (1, 2), (3, 2), (2, 1), (2, 3), (2, 2),
]
EARLY = 7 * 16
FAR_FIRST = (2, 1, 3)
NEAR_FIRST = (1, 3, 2)


def along(axis, d):
    return (d, 0) if axis == 0 else (0, d)


def slot(place):
    return ORDER.index((place[0] % 4, place[1] % 4))


GATHER = []
for axis in (0, 1):
    GATHER += [(axis, (0, 0), along(axis, d)) for d in FAR_FIRST]
for axis in (0, 1):
    GATHER += [(1 - axis, (0, 0), along(axis, d)) for d in FAR_FIRST]
FORWARD = []
for d in NEAR_FIRST:
    for axis in (0, 1):
        first = GATHER.index((axis, (0, 0), along(axis, d)))
        after = [(axis, along(axis, -d % 4), along(1 - axis, e)) for e in FAR_FIRST]
        FORWARD.append((first, range(len(GATHER), len(GATHER) + 3)))
        GATHER += after


def rms_unit(values):
    return values * lax.rsqrt(jnp.mean(values * values, axis=-1, keepdims=True) + 1e-06)


def kernel(
    lat, pn, bidx, off, scl, gate, upq, upf, dnt, cache_hbm, wqkv_hbm, wffn_hbm, woa_hbm, wof_hbm,
    out,
    win, wout, cachev, skv, r1, kv, xin, xg, qkv, act, part, rb, tb, r2,
    ag_s, ag_r, rs_s, rs_r, st_s, st_r, x_s, x_r, w_sem,
):
    patches = xin.shape[0]
    sections = lax.axis_size("section")
    sec = lax.axis_index("section")
    head = lax.axis_index("head")
    x = head // 4
    y = lax.rem(head, 4)

    def px(d):
        return lax.rem(x + (d + 4), 4)

    def py(d):
        return lax.rem(y + (d + 4), 4)

    def dev(d):
        return (sec, px(d[0]) * 4 + py(d[1]))

    first_section = sec == 0
    last_section = sec == sections - 1

    w_copies = [
        pltpu.make_async_copy(cache_hbm, cachev, w_sem.at[0]),
        pltpu.make_async_copy(wqkv_hbm.at[0], win.at[:, pl.ds(0, DH)], w_sem.at[1]),
        pltpu.make_async_copy(wqkv_hbm.at[1], win.at[:, pl.ds(DH, DH)], w_sem.at[2]),
        pltpu.make_async_copy(wqkv_hbm.at[2], win.at[:, pl.ds(2 * DH, DH)], w_sem.at[3]),
        pltpu.make_async_copy(wffn_hbm, win.at[:, pl.ds(3 * DH, 768)], w_sem.at[4]),
        pltpu.make_async_copy(woa_hbm, wout.at[pl.ds(0, DH)], w_sem.at[5]),
        pltpu.make_async_copy(wof_hbm, wout.at[pl.ds(DH, 768)], w_sem.at[6]),
    ]
    w_copies[0].start()

    barrier = pltpu.get_barrier_semaphore()
    for d in FAR_FIRST:
        for axis in (0, 1):
            pl.semaphore_signal(
                barrier, inc=1, device_id=dev(along(axis, d)), device_id_type=MESH
            )
    for step in (1, sections - 1):
        neighbour = (lax.rem(sec + step, sections), head)
        pl.semaphore_signal(barrier, inc=1, device_id=neighbour, device_id_type=MESH)
    pl.semaphore_wait(barrier, 8)

    def remote(src, dst, ssem, rsem, device):
        return pltpu.make_async_remote_copy(
            src_ref=src, dst_ref=dst, send_sem=ssem, recv_sem=rsem, device_id=device,
            device_id_type=MESH,
        )

    def gather_copy(m, i):
        hf, place, way = GATHER[i]
        there = slot((place[0] - way[0], place[1] - way[1]))
        return remote(
            xg.at[m, hf, slot(place)], xg.at[m, hf, there], ag_s.at[m, i], ag_r.at[m, i], dev(way)
        )

    def gather_landed(m, i):
        hf, place, way = GATHER[i]
        ref = xg.at[m, hf, slot((place[0] - way[0], place[1] - way[1]))]
        remote(ref, ref, ag_s.at[m, i], ag_r.at[m, i], dev((-way[0], -way[1]))).wait_recv()

    def stale_first(m, i):
        if i < 3:
            d = (1, -1, 2)[i]
            return remote(
                skv.at[m, 0, px(d)], r1.at[m, 0, x], st_s.at[m, i], st_r.at[m, i], dev((d, 0))
            )
        d = (1, -1, 2)[i - 3]
        return remote(
            skv.at[m, 1, py(d)], r1.at[m, 1, y], st_s.at[m, i], st_r.at[m, i], dev((0, d))
        )

    def stale_first_landed(m, i):
        if i < 3:
            d = (-1, 1, 2)[i]
            ref, device = r1.at[m, 0, px(d)], dev((d, 0))
        else:
            d = (-1, 1, 2)[i - 3]
            ref, device = r1.at[m, 1, py(d)], dev((0, d))
        remote(ref, ref, st_s.at[m, i], st_r.at[m, i], device).wait_recv()

    def stale_second(m, i):
        if i < 9:
            d = (1, -1, 2)[i - 6]
            return remote(
                r1.at[m, 0, :, py(d)], kv.at[m, 0, y], st_s.at[m, i], st_r.at[m, i], dev((0, d))
            )
        d = (1, -1, 2)[i - 9]
        return remote(
            r1.at[m, 1, :, px(d)], kv.at[m, 1, x], st_s.at[m, i], st_r.at[m, i], dev((d, 0))
        )

    def stale_second_landed(m, i):
        if i < 9:
            d = (-1, 1, 2)[i - 6]
            ref, device = kv.at[m, 0, py(d)], dev((0, d))
        else:
            d = (-1, 1, 2)[i - 9]
            ref, device = kv.at[m, 1, px(d)], dev((d, 0))
        remote(ref, ref, st_s.at[m, i], st_r.at[m, i], device).wait_recv()

    def stale_send(m):
        def one(j, _):
            block = bidx[m, 0, j]
            both = cachev[block]
            keys = both[:, 0].astype(F32)
            values = both[:, 1]
            rows = pl.ds(pl.multiple_of(j * 16, 16), 16)
            for h in range(16):
                part_k = keys[:, h * DH:(h + 1) * DH]
                skv[m, 0, h // 4, h % 4, rows, :] = rms_unit(part_k).astype(BF16)
                skv[m, 1, h % 4, h // 4, rows, :] = values[:, h * DH:(h + 1) * DH]
            return 0

        lax.fori_loop(0, 4, one, 0)
        for i in range(6):
            stale_first(m, i).start()
        r1[m, 0, x] = skv[m, 0, x]
        r1[m, 1, y] = skv[m, 1, y]

    def stale_forward(m):
        for i in range(3):
            stale_first_landed(m, i)
        for i in range(6, 9):
            stale_second(m, i).start()
        for i in range(3, 6):
            stale_first_landed(m, i)
        for i in range(9, 12):
            stale_second(m, i).start()
        kv[m, 0, y] = r1[m, 0, :, y]
        kv[m, 1, x] = r1[m, 1, :, x]

    def sum_way(i):
        second, c, d = i // 12, i % 12 // 3, FAR_FIRST[i % 3]
        return c, d, along((1 - c % 2) if second == 0 else c % 2, d)

    def sum_copy(m, i):
        c, d, way = sum_way(i)
        if i < 12:
            source = part.at[m, c, :, d] if c % 2 == 0 else part.at[m, c, d]
            target = rb.at[m, i]
        else:
            source, target = tb.at[m, c, d], r2.at[m, i - 12]
        return remote(source, target, rs_s.at[m, i], rs_r.at[m, i], dev(way))

    def sum_landed(m, i):
        _, _, way = sum_way(i)
        target = rb.at[m, i] if i < 12 else r2.at[m, i - 12]
        remote(
            target, target, rs_s.at[m, i], rs_r.at[m, i], dev((-way[0], -way[1]))
        ).wait_recv()

    def hand_on(m, c):
        cols = pl.ds(c * 768, 768)
        return remote(
            out.at[m, :, cols], xin.at[m, :, cols], x_s.at[m, c], x_r.at[m, c], (sec + 1, head)
        )

    def handed(m, c):
        ref = xin.at[m, :, pl.ds(c * 768, 768)]
        remote(ref, ref, x_s.at[m, c], x_r.at[m, c], (sec - 1, head)).wait_recv()

    def modulate_and_send(m):
        @pl.when(first_section)
        def _():
            xin[m] = lat[pn[m]]

        @pl.when(sec > 0)
        def _():
            for c in range(4):
                handed(m, c)

        values = xin[m].astype(F32)
        center = values - jnp.mean(values, axis=-1, keepdims=True)
        spread = jnp.mean(center * center, axis=-1, keepdims=True)
        normed = center * lax.rsqrt(spread + 1e-06)
        modded = (normed * (1.0 + scl[...]) + off[...]).astype(BF16)
        xg[m, A, 0] = modded[:, :1536]
        xg[m, B, 0] = modded[:, 1536:]
        for i in range(12):
            gather_copy(m, i).start()

    def gather_forward(m):
        for first, after in FORWARD:
            gather_landed(m, first)
            for i in after:
                gather_copy(m, i).start()
        for i in range(6, 12):
            gather_landed(m, i)

    def gather_rest(m):
        for i in range(12, len(GATHER)):
            gather_landed(m, i)

    def dot(a, b):
        return jnp.dot(a, b, preferred_element_type=F32)

    def dot_tn(a, b):
        return lax.dot_general(a, b, (((0,), (0,)), ((), ())), preferred_element_type=F32)

    def dot_nt(a, b):
        return lax.dot_general(a, b, (((1,), (1,)), ((), ())), preferred_element_type=F32)

    def merge(i, _):
        rows = pl.ds(pl.multiple_of(i * 256, 256), 256)
        down = dnt[:, rows]
        for n in range(3):
            win[rows, n * DH:(n + 1) * DH] = (
                win[rows, n * DH:(n + 1) * DH].astype(F32) + dot_tn(down, upq[n])
            ).astype(BF16)
            cols = slice(3 * DH + n * 256, 3 * DH + (n + 1) * 256)
            win[rows, cols] = (
                win[rows, cols].astype(F32) + dot_tn(down, upf[:, n * 256:(n + 1) * 256])
            ).astype(BF16)
        return 0

    def project(m, lo, hi):
        def tile(first, width):
            acc = None
            for hf in range(2):
                rows = xg[m, hf, lo // 16:hi // 16].reshape(hi - lo, 1536)
                term = dot(rows, win[hf * 1536:(hf + 1) * 1536, pl.ds(first, width)])
                acc = term if acc is None else acc + term
            return acc

        qkv[lo:hi, 0:256] = tile(0, 256)
        qkv[lo:hi, 256:384] = tile(256, DH)

        def feed(n, _):
            cols = pl.ds(pl.multiple_of(n * 256 + DH, DH), 256)
            acc = tile(pl.multiple_of(n * 256 + 3 * DH, DH), 256)
            act[lo:hi, cols] = jax.nn.gelu(acc, approximate=True).astype(BF16)
            return 0

        lax.fori_loop(0, 3, feed, 0)

    def attend_to(queries, keys, values, state):
        expo = jnp.exp(dot_nt(queries, keys) * (1.0 / math.sqrt(DH)))
        total = jnp.sum(expo, axis=-1, keepdims=True)
        mixed = dot(expo.astype(BF16), values)
        return (mixed, total) if state is None else (state[0] + mixed, state[1] + total)

    def attend_cached(m, lo, hi):
        queries = rms_unit(qkv[lo:hi, 0:DH]).astype(BF16)
        state = None
        for j in range(4):
            keys = kv[m, 0, j].reshape(256, DH)
            values = kv[m, 1, :, j].reshape(256, DH)
            state = attend_to(queries, keys, values, state)
        return queries, state

    def attend_fresh(early, late):
        keys = rms_unit(qkv[:, DH:2 * DH]).astype(BF16)
        values = qkv[:, 2 * DH:3 * DH].astype(BF16)
        for lo, hi, (queries, state) in ((0, EARLY, early), (EARLY, 256, late)):
            mixed, total = attend_to(queries, keys, values, state)
            act[lo:hi, 0:DH] = (mixed / total).astype(BF16)

    def output_products(m):
        for c in range(4):
            for n in range(3):
                lo = c * 768 + n * 256
                term = dot(act[...], wout[:, lo:lo + 256]).astype(BF16)
                for k, place in enumerate(ORDER):
                    rows = term[k * 16:(k + 1) * 16]
                    part[m, c, place[0], place[1], :, n * 256:(n + 1) * 256] = rows
            for j in range(3):
                sum_copy(m, 3 * c + j).start()

    def wide(value):
        return value.astype(F32)

    def sum_up(m):
        for c in range(4):
            total = wide(part[m, c, :, 0] if c % 2 == 0 else part[m, c, 0])
            for j in range(3):
                sum_landed(m, 3 * c + j)
                total += wide(rb[m, 3 * c + j])
            tb[m, c] = total.astype(BF16)
            for j in range(3):
                sum_copy(m, 12 + 3 * c + j).start()
        for c in range(4):
            branch = wide(part[m, c, 0, 0])
            for j in range(3):
                branch += wide(rb[m, 3 * c + j, 0])
            for j in range(3):
                sum_landed(m, 12 + 3 * c + j)
                branch += wide(r2[m, 3 * c + j])
            cols = slice(c * 768, (c + 1) * 768)
            out[m, :, cols] = (wide(xin[m, :, cols]) + gate[:, cols] * branch).astype(BF16)

            @pl.when(sec < sections - 1)
            def _():
                hand_on(m, c).start()

    def stale_send_step(m, _):
        stale_send(m)
        return 0

    def stale_forward_step(m, _):
        stale_forward(m)
        return 0

    @pl.when(sec > 0)
    def _():
        w_copies[0].wait()
        for copy in w_copies[1:]:
            copy.start()
        lax.fori_loop(0, patches, stale_send_step, 0)
        for copy in w_copies[1:5]:
            copy.wait()
        lax.fori_loop(0, 12, merge, 0)
        lax.fori_loop(0, patches, stale_forward_step, 0)

    def patch(m, _):
        opening = jnp.logical_and(sec == 0, m == 0)
        modulate_and_send(m)

        @pl.when(opening)
        def _():
            w_copies[0].wait()
            for copy in w_copies[1:]:
                copy.start()
            stale_send(0)

        gather_forward(m)

        @pl.when(opening)
        def _():
            for copy in w_copies[1:5]:
                copy.wait()
            lax.fori_loop(0, 12, merge, 0)
            stale_forward(0)

        project(m, 0, EARLY)
        for i in range(6, 12):
            stale_second_landed(m, i)
        early = attend_cached(m, 0, EARLY)
        gather_rest(m)
        project(m, EARLY, 256)

        @pl.when(opening)
        def _():
            lax.fori_loop(1, patches, stale_send_step, 0)

        late = attend_cached(m, EARLY, 256)
        attend_fresh(early, late)

        @pl.when(m == 0)
        def _():
            for copy in w_copies[5:]:
                copy.wait()

        output_products(m)

        @pl.when(opening)
        def _():
            lax.fori_loop(1, patches, stale_forward_step, 0)

        sum_up(m)
        return 0

    lax.fori_loop(0, patches, patch, 0)

    def drain(m, _):
        for i in range(len(GATHER)):
            gather_copy(m, i).wait_send()
        for i in range(24):
            sum_copy(m, i).wait_send()
        for i in range(6):
            stale_first(m, i).wait_send()
        for i in range(6, 12):
            stale_second(m, i).wait_send()

        @pl.when(sec < sections - 1)
        def _():
            for c in range(4):
                hand_on(m, c).wait_send()

        return 0

    lax.fori_loop(0, patches, drain, 0)


def per_device(
    latents, patch_numbers, prior_step_cache, old_block_index, modulation_offset, modulation_scale,
    modulation_gate, query_key_value_weight, feedforward_input_weight, adapter_down_weight,
    adapter_up_query_key_value, adapter_up_feedforward, attention_output_weight,
    feedforward_output_weight,
):
    patches = old_block_index.shape[1]
    vmem = pl.BlockSpec(memory_space=pltpu.VMEM)
    smem = pl.BlockSpec(memory_space=pltpu.SMEM)
    hbm = pl.BlockSpec(memory_space=pl.ANY)
    dma = pltpu.SemaphoreType.DMA
    record = pl.pallas_call(
        kernel,
        out_shape=jax.ShapeDtypeStruct((patches, 16, 3072), BF16),
        in_specs=[vmem, smem, smem] + [vmem] * 6 + [hbm] * 5,
        out_specs=vmem,
        scratch_shapes=[
            pltpu.VMEM((3072, 1152), BF16),
            pltpu.VMEM((896, 3072), BF16),
            pltpu.VMEM((16, 16, 2, 2048), BF16),
            pltpu.VMEM((patches, 2, 4, 4, 64, DH), BF16),
            pltpu.VMEM((patches, 2, 4, 4, 64, DH), BF16),
            pltpu.VMEM((patches, 2, 4, 4, 64, DH), BF16),
            pltpu.VMEM((patches, 16, 3072), BF16),
            pltpu.VMEM((patches, 2, 16, 16, 1536), BF16),
            pltpu.VMEM((256, 3 * DH), F32),
            pltpu.VMEM((256, 896), BF16),
            pltpu.VMEM((patches, 4, 4, 4, 16, 768), BF16),
            pltpu.VMEM((patches, 12, 4, 16, 768), BF16),
            pltpu.VMEM((patches, 4, 4, 16, 768), BF16),
            pltpu.VMEM((patches, 12, 16, 768), BF16),
            dma((patches, len(GATHER))),
            dma((patches, len(GATHER))),
            dma((patches, 24)),
            dma((patches, 24)),
            dma((patches, 12)),
            dma((patches, 12)),
            dma((patches, 4)),
            dma((patches, 4)),
            dma((7,)),
        ],
        compiler_params=pltpu.CompilerParams(
            collective_id=0, has_side_effects=True, vmem_limit_bytes=58 * 2**20
        ),
        cost_estimate=pl.CostEstimate(
            flops=10_000_000_000, bytes_accessed=16_000_000, transcendentals=2_000_000
        ),
    )(
        latents,
        patch_numbers,
        old_block_index.transpose(1, 0, 2),
        modulation_offset,
        modulation_scale,
        modulation_gate,
        adapter_up_query_key_value[0].transpose(1, 0, 2),
        adapter_up_feedforward[0],
        adapter_down_weight[0].T,
        prior_step_cache[0],
        query_key_value_weight[0].transpose(1, 0, 2),
        feedforward_input_weight[0],
        attention_output_weight[0],
        feedforward_output_weight[0],
    )
    return record[None]


def solution(mesh):
    placed = (
        P(None, "head", None),
        P(),
        P("section", None, "head", None, None),
        P("section", None, None),
        P("section", None),
        P("section", None),
        P("section", None),
        P("section", None, None, "head"),
        P("section", None, "head"),
        P("section", None, None),
        P("section", None, None, "head"),
        P("section", None, "head"),
        P("section", "head", None),
        P("section", "head", None),
    )
    return jax.shard_map(
        per_device,
        mesh=mesh,
        in_specs=placed,
        out_specs=P("section", None, "head", None),
        check_vma=False,
    )
```

```python
import math

import jax
import jax.numpy as jnp
from jax import lax
from jax.experimental import pallas as pl
from jax.experimental.pallas import tpu as pltpu
from jax.sharding import PartitionSpec as P

DH = 128
MESH = pl.DeviceIdType.MESH
F32 = jnp.float32
BF16 = jnp.bfloat16
A, B = 0, 1

ORDER = [
    (0, 0), (1, 0), (3, 0), (2, 0), (0, 1), (0, 3), (0, 2),
    (1, 1), (1, 3), (3, 1), (3, 3), (1, 2), (3, 2), (2, 1), (2, 3), (2, 2),
]
EARLY = 7 * 16
FAR_FIRST = (2, 1, 3)
NEAR_FIRST = (1, 3, 2)


def along(axis, d):
    return (d, 0) if axis == 0 else (0, d)


def slot(place):
    return ORDER.index((place[0] % 4, place[1] % 4))


GATHER = []
for axis in (0, 1):
    GATHER += [(axis, (0, 0), along(axis, d)) for d in FAR_FIRST]
for axis in (0, 1):
    GATHER += [(1 - axis, (0, 0), along(axis, d)) for d in FAR_FIRST]
FORWARD = []
for d in NEAR_FIRST:
    for axis in (0, 1):
        first = GATHER.index((axis, (0, 0), along(axis, d)))
        after = [(axis, along(axis, -d % 4), along(1 - axis, e)) for e in FAR_FIRST]
        FORWARD.append((first, range(len(GATHER), len(GATHER) + 3)))
        GATHER += after


def rms_unit(values):
    return values * lax.rsqrt(jnp.mean(values * values, axis=-1, keepdims=True) + 1e-06)


def kernel(
    pn, bidx, lat_hbm, off_hbm, scl_hbm, gate_hbm, upq_hbm, upf_hbm, dnt_hbm, cache_hbm, wqkv_hbm,
    wffn_hbm, woa_hbm, wof_hbm,
    out,
    lat, off, scl, gate, upq, upf, dnt,
    win, wout, cachev, skv, r1, kv, xin, xg, qkv, act, part, rb, tb, r2,
    ag_s, ag_r, rs_s, rs_r, st_s, st_r, x_s, x_r, w_sem, turn,
):
    patches = xin.shape[0]
    sections = lax.axis_size("section")
    sec = lax.axis_index("section")
    head = lax.axis_index("head")
    x = head // 4
    y = lax.rem(head, 4)

    def px(d):
        return lax.rem(x + (d + 4), 4)

    def py(d):
        return lax.rem(y + (d + 4), 4)

    def dev(d):
        return (sec, px(d[0]) * 4 + py(d[1]))

    first_section = sec == 0
    last_section = sec == sections - 1

    w_copies = [
        pltpu.make_async_copy(cache_hbm, cachev, w_sem.at[0]),
        pltpu.make_async_copy(wqkv_hbm.at[0], win.at[:, pl.ds(0, DH)], w_sem.at[1]),
        pltpu.make_async_copy(wqkv_hbm.at[1], win.at[:, pl.ds(DH, DH)], w_sem.at[2]),
        pltpu.make_async_copy(wqkv_hbm.at[2], win.at[:, pl.ds(2 * DH, DH)], w_sem.at[3]),
        pltpu.make_async_copy(wffn_hbm, win.at[:, pl.ds(3 * DH, 768)], w_sem.at[4]),
        pltpu.make_async_copy(woa_hbm, wout.at[pl.ds(0, DH)], w_sem.at[5]),
        pltpu.make_async_copy(wof_hbm, wout.at[pl.ds(DH, 768)], w_sem.at[6]),
    ]
    v_copies = [
        pltpu.make_async_copy(source, target, w_sem.at[7 + i])
        for i, (source, target) in enumerate((
            (off_hbm, off), (scl_hbm, scl), (gate_hbm, gate), (upq_hbm, upq), (upf_hbm, upf),
            (dnt_hbm, dnt), (lat_hbm, lat),
        ))
    ]

    @pl.when(first_section)
    def _():
        v_copies[6].start()

    for copy in v_copies[:3]:
        copy.start()
    w_copies[0].start()
    for copy in v_copies[3:6]:
        copy.start()

    barrier = pltpu.get_barrier_semaphore()
    for d in FAR_FIRST:
        for axis in (0, 1):
            pl.semaphore_signal(
                barrier, inc=1, device_id=dev(along(axis, d)), device_id_type=MESH
            )
    for step in (1, sections - 1):
        neighbour = (lax.rem(sec + step, sections), head)
        pl.semaphore_signal(barrier, inc=1, device_id=neighbour, device_id_type=MESH)
    pl.semaphore_wait(barrier, 8)

    def remote(src, dst, ssem, rsem, device):
        return pltpu.make_async_remote_copy(
            src_ref=src, dst_ref=dst, send_sem=ssem, recv_sem=rsem, device_id=device,
            device_id_type=MESH,
        )

    def gather_copy(m, i):
        hf, place, way = GATHER[i]
        there = slot((place[0] - way[0], place[1] - way[1]))
        return remote(
            xg.at[m, hf, slot(place)], xg.at[m, hf, there], ag_s.at[m, i], ag_r.at[m, i], dev(way)
        )

    def gather_landed(m, i):
        hf, place, way = GATHER[i]
        ref = xg.at[m, hf, slot((place[0] - way[0], place[1] - way[1]))]
        remote(ref, ref, ag_s.at[m, i], ag_r.at[m, i], dev((-way[0], -way[1]))).wait_recv()

    def stale_first(m, i):
        if i < 3:
            d = (1, -1, 2)[i]
            return remote(
                skv.at[m, 0, px(d)], r1.at[m, 0, x], st_s.at[m, i], st_r.at[m, i], dev((d, 0))
            )
        d = (1, -1, 2)[i - 3]
        return remote(
            skv.at[m, 1, py(d)], r1.at[m, 1, y], st_s.at[m, i], st_r.at[m, i], dev((0, d))
        )

    def stale_first_landed(m, i):
        if i < 3:
            d = (-1, 1, 2)[i]
            ref, device = r1.at[m, 0, px(d)], dev((d, 0))
        else:
            d = (-1, 1, 2)[i - 3]
            ref, device = r1.at[m, 1, py(d)], dev((0, d))
        remote(ref, ref, st_s.at[m, i], st_r.at[m, i], device).wait_recv()

    def stale_second(m, i):
        if i < 9:
            d = (1, -1, 2)[i - 6]
            return remote(
                r1.at[m, 0, :, py(d)], kv.at[m, 0, y], st_s.at[m, i], st_r.at[m, i], dev((0, d))
            )
        d = (1, -1, 2)[i - 9]
        return remote(
            r1.at[m, 1, :, px(d)], kv.at[m, 1, x], st_s.at[m, i], st_r.at[m, i], dev((d, 0))
        )

    def stale_second_landed(m, i):
        if i < 9:
            d = (-1, 1, 2)[i - 6]
            ref, device = kv.at[m, 0, py(d)], dev((0, d))
        else:
            d = (-1, 1, 2)[i - 9]
            ref, device = kv.at[m, 1, px(d)], dev((d, 0))
        remote(ref, ref, st_s.at[m, i], st_r.at[m, i], device).wait_recv()

    def stale_send(m):
        def one(j, _):
            block = bidx[m, 0, j]
            both = cachev[block]
            keys = both[:, 0].astype(F32)
            values = both[:, 1]
            rows = pl.ds(pl.multiple_of(j * 16, 16), 16)
            for h in range(16):
                part_k = keys[:, h * DH:(h + 1) * DH]
                skv[m, 0, h // 4, h % 4, rows, :] = rms_unit(part_k).astype(BF16)
                skv[m, 1, h % 4, h // 4, rows, :] = values[:, h * DH:(h + 1) * DH]
            return 0

        lax.fori_loop(0, 4, one, 0)
        for i in range(6):
            stale_first(m, i).start()
        r1[m, 0, x] = skv[m, 0, x]
        r1[m, 1, y] = skv[m, 1, y]

    def stale_forward(m):
        for i in range(3):
            stale_first_landed(m, i)
        for i in range(6, 9):
            stale_second(m, i).start()
        for i in range(3, 6):
            stale_first_landed(m, i)
        for i in range(9, 12):
            stale_second(m, i).start()
        kv[m, 0, y] = r1[m, 0, :, y]
        kv[m, 1, x] = r1[m, 1, :, x]

    def sum_way(i):
        second, c, d = i // 12, i % 12 // 3, FAR_FIRST[i % 3]
        return c, d, along((1 - c % 2) if second == 0 else c % 2, d)

    def sum_copy(m, i):
        c, d, way = sum_way(i)
        if i < 12:
            source = part.at[m, c, :, d] if c % 2 == 0 else part.at[m, c, d]
            target = rb.at[m, i]
        else:
            source, target = tb.at[m, c, d], r2.at[m, i - 12]
        return remote(source, target, rs_s.at[m, i], rs_r.at[m, i], dev(way))

    def sum_landed(m, i):
        _, _, way = sum_way(i)
        target = rb.at[m, i] if i < 12 else r2.at[m, i - 12]
        remote(
            target, target, rs_s.at[m, i], rs_r.at[m, i], dev((-way[0], -way[1]))
        ).wait_recv()

    def hand_on(m, c):
        cols = pl.ds(c * 768, 768)
        return remote(
            out.at[m, :, cols], xin.at[m, :, cols], x_s.at[m, c], x_r.at[m, c], (sec + 1, head)
        )

    def handed(m, c):
        ref = xin.at[m, :, pl.ds(c * 768, 768)]
        remote(ref, ref, x_s.at[m, c], x_r.at[m, c], (sec - 1, head)).wait_recv()

    def modulate_and_send(m):
        @pl.when(first_section)
        def _():
            xin[m] = lat[pn[m]]

        @pl.when(sec > 0)
        def _():
            for c in range(4):
                handed(m, c)

        values = xin[m].astype(F32)
        center = values - jnp.mean(values, axis=-1, keepdims=True)
        spread = jnp.mean(center * center, axis=-1, keepdims=True)
        normed = center * lax.rsqrt(spread + 1e-06)
        modded = (normed * (1.0 + scl[...]) + off[...]).astype(BF16)
        xg[m, A, 0] = modded[:, :1536]
        xg[m, B, 0] = modded[:, 1536:]
        for i in range(12):
            gather_copy(m, i).start()

    def gather_forward(m):
        for first, after in FORWARD:
            gather_landed(m, first)
            for i in after:
                gather_copy(m, i).start()
        for i in range(6, 12):
            gather_landed(m, i)

    def gather_rest(m):
        for i in range(12, len(GATHER)):
            gather_landed(m, i)

    def dot(a, b):
        return jnp.dot(a, b, preferred_element_type=F32)

    def dot_tn(a, b):
        return lax.dot_general(a, b, (((0,), (0,)), ((), ())), preferred_element_type=F32)

    def dot_nt(a, b):
        return lax.dot_general(a, b, (((1,), (1,)), ((), ())), preferred_element_type=F32)

    def merge(i, _):
        rows = pl.ds(pl.multiple_of(i * 256, 256), 256)
        down = dnt[:, rows]
        for n in range(3):
            win[rows, n * DH:(n + 1) * DH] = (
                win[rows, n * DH:(n + 1) * DH].astype(F32) + dot_tn(down, upq[n])
            ).astype(BF16)
            cols = slice(3 * DH + n * 256, 3 * DH + (n + 1) * 256)
            win[rows, cols] = (
                win[rows, cols].astype(F32) + dot_tn(down, upf[:, n * 256:(n + 1) * 256])
            ).astype(BF16)
        return 0

    def project(m, lo, hi):
        def tile(first, width):
            acc = None
            for hf in range(2):
                rows = xg[m, hf, lo // 16:hi // 16].reshape(hi - lo, 1536)
                term = dot(rows, win[hf * 1536:(hf + 1) * 1536, pl.ds(first, width)])
                acc = term if acc is None else acc + term
            return acc

        qkv[lo:hi, 0:256] = tile(0, 256)
        qkv[lo:hi, 256:384] = tile(256, DH)

        def feed(n, _):
            cols = pl.ds(pl.multiple_of(n * 256 + DH, DH), 256)
            acc = tile(pl.multiple_of(n * 256 + 3 * DH, DH), 256)
            act[lo:hi, cols] = jax.nn.gelu(acc, approximate=True).astype(BF16)
            return 0

        lax.fori_loop(0, 3, feed, 0)

    def attend_to(queries, keys, values, state):
        expo = jnp.exp(dot_nt(queries, keys) * (1.0 / math.sqrt(DH)))
        total = jnp.sum(expo, axis=-1, keepdims=True)
        mixed = dot(expo.astype(BF16), values)
        return (mixed, total) if state is None else (state[0] + mixed, state[1] + total)

    def attend_cached(m, lo, hi):
        queries = rms_unit(qkv[lo:hi, 0:DH]).astype(BF16)
        state = None
        for j in range(4):
            keys = kv[m, 0, j].reshape(256, DH)
            values = kv[m, 1, :, j].reshape(256, DH)
            state = attend_to(queries, keys, values, state)
        return queries, state

    def attend_fresh(early, late):
        keys = rms_unit(qkv[:, DH:2 * DH]).astype(BF16)
        values = qkv[:, 2 * DH:3 * DH].astype(BF16)
        for lo, hi, (queries, state) in ((0, EARLY, early), (EARLY, 256, late)):
            mixed, total = attend_to(queries, keys, values, state)
            act[lo:hi, 0:DH] = (mixed / total).astype(BF16)

    def output_products(m):
        for c in range(4):
            for n in range(3):
                lo = c * 768 + n * 256
                term = dot(act[...], wout[:, lo:lo + 256]).astype(BF16)
                for k, place in enumerate(ORDER):
                    rows = term[k * 16:(k + 1) * 16]
                    part[m, c, place[0], place[1], :, n * 256:(n + 1) * 256] = rows
            for j in range(3):
                sum_copy(m, 3 * c + j).start()

    def wide(value):
        return value.astype(F32)

    def sum_up(m):
        for c in range(4):
            total = wide(part[m, c, :, 0] if c % 2 == 0 else part[m, c, 0])
            for j in range(3):
                sum_landed(m, 3 * c + j)
                total += wide(rb[m, 3 * c + j])
            tb[m, c] = total.astype(BF16)
            for j in range(3):
                sum_copy(m, 12 + 3 * c + j).start()
        for c in range(4):
            branch = wide(part[m, c, 0, 0])
            for j in range(3):
                branch += wide(rb[m, 3 * c + j, 0])
            for j in range(3):
                sum_landed(m, 12 + 3 * c + j)
                branch += wide(r2[m, 3 * c + j])
            cols = slice(c * 768, (c + 1) * 768)
            out[m, :, cols] = (wide(xin[m, :, cols]) + gate[:, cols] * branch).astype(BF16)

            @pl.when(sec < sections - 1)
            def _():
                hand_on(m, c).start()

    def stale_send_step(m, _):
        stale_send(m)
        return 0

    def stale_forward_step(m, _):
        stale_forward(m)
        return 0

    @pl.when(sec > 0)
    def _():
        w_copies[0].wait()
        for copy in w_copies[1:]:
            copy.start()
        lax.fori_loop(0, patches, stale_send_step, 0)
        for copy in w_copies[1:5] + v_copies[:6]:
            copy.wait()
        lax.fori_loop(0, 12, merge, 0)
        lax.fori_loop(0, patches, stale_forward_step, 0)

    @pl.when(first_section)
    def _():
        for copy in v_copies[:3] + v_copies[6:]:
            copy.wait()

    def await_turn(m):
        @pl.when(jnp.logical_and(lax.rem(sec, 2) == 0, m > 0))
        def _():
            pl.semaphore_wait(turn, 1)

    def give_turn(m):
        @pl.when(jnp.logical_and(lax.rem(sec, 2) == 1, m < patches - 1))
        def _():
            pl.semaphore_signal(turn, inc=1, device_id=(sec - 1, head), device_id_type=MESH)

    def patch(m, _):
        opening = jnp.logical_and(sec == 0, m == 0)
        await_turn(m)
        modulate_and_send(m)

        @pl.when(opening)
        def _():
            w_copies[0].wait()
            for copy in w_copies[1:]:
                copy.start()
            stale_send(0)

        gather_forward(m)
        give_turn(m)

        @pl.when(opening)
        def _():
            for copy in w_copies[1:5] + v_copies[3:6]:
                copy.wait()
            lax.fori_loop(0, 12, merge, 0)
            stale_forward(0)

        project(m, 0, EARLY)
        for i in range(6, 12):
            stale_second_landed(m, i)
        early = attend_cached(m, 0, EARLY)
        gather_rest(m)
        project(m, EARLY, 256)

        @pl.when(opening)
        def _():
            lax.fori_loop(1, patches, stale_send_step, 0)

        late = attend_cached(m, EARLY, 256)
        attend_fresh(early, late)

        @pl.when(m == 0)
        def _():
            for copy in w_copies[5:]:
                copy.wait()

        output_products(m)

        @pl.when(opening)
        def _():
            lax.fori_loop(1, patches, stale_forward_step, 0)

        sum_up(m)
        return 0

    lax.fori_loop(0, patches, patch, 0)

    def drain(m, _):
        for i in range(len(GATHER)):
            gather_copy(m, i).wait_send()
        for i in range(24):
            sum_copy(m, i).wait_send()
        for i in range(6):
            stale_first(m, i).wait_send()
        for i in range(6, 12):
            stale_second(m, i).wait_send()

        @pl.when(sec < sections - 1)
        def _():
            for c in range(4):
                hand_on(m, c).wait_send()

        return 0

    lax.fori_loop(0, patches, drain, 0)


def per_device(
    latents, patch_numbers, prior_step_cache, old_block_index, modulation_offset, modulation_scale,
    modulation_gate, query_key_value_weight, feedforward_input_weight, adapter_down_weight,
    adapter_up_query_key_value, adapter_up_feedforward, attention_output_weight,
    feedforward_output_weight,
):
    patches = old_block_index.shape[1]
    vmem = pl.BlockSpec(memory_space=pltpu.VMEM)
    smem = pl.BlockSpec(memory_space=pltpu.SMEM)
    hbm = pl.BlockSpec(memory_space=pl.ANY)
    dma = pltpu.SemaphoreType.DMA
    record = pl.pallas_call(
        kernel,
        out_shape=jax.ShapeDtypeStruct((patches, 16, 3072), BF16),
        in_specs=[smem, smem] + [hbm] * 12,
        out_specs=vmem,
        scratch_shapes=[
            pltpu.VMEM(latents.shape, BF16),
            pltpu.VMEM((1, 3072), F32),
            pltpu.VMEM((1, 3072), F32),
            pltpu.VMEM((1, 3072), F32),
            pltpu.VMEM((3, 64, DH), BF16),
            pltpu.VMEM((64, 768), BF16),
            pltpu.VMEM((64, 3072), BF16),
            pltpu.VMEM((3072, 1152), BF16),
            pltpu.VMEM((896, 3072), BF16),
            pltpu.VMEM((16, 16, 2, 2048), BF16),
            pltpu.VMEM((patches, 2, 4, 4, 64, DH), BF16),
            pltpu.VMEM((patches, 2, 4, 4, 64, DH), BF16),
            pltpu.VMEM((patches, 2, 4, 4, 64, DH), BF16),
            pltpu.VMEM((patches, 16, 3072), BF16),
            pltpu.VMEM((patches, 2, 16, 16, 1536), BF16),
            pltpu.VMEM((256, 3 * DH), F32),
            pltpu.VMEM((256, 896), BF16),
            pltpu.VMEM((patches, 4, 4, 4, 16, 768), BF16),
            pltpu.VMEM((patches, 12, 4, 16, 768), BF16),
            pltpu.VMEM((patches, 4, 4, 16, 768), BF16),
            pltpu.VMEM((patches, 12, 16, 768), BF16),
            dma((patches, len(GATHER))),
            dma((patches, len(GATHER))),
            dma((patches, 24)),
            dma((patches, 24)),
            dma((patches, 12)),
            dma((patches, 12)),
            dma((patches, 4)),
            dma((patches, 4)),
            dma((14,)),
            pltpu.SemaphoreType.REGULAR,
        ],
        compiler_params=pltpu.CompilerParams(
            collective_id=0, has_side_effects=True, vmem_limit_bytes=58 * 2**20
        ),
        cost_estimate=pl.CostEstimate(
            flops=10_000_000_000, bytes_accessed=16_000_000, transcendentals=2_000_000
        ),
    )(
        patch_numbers,
        old_block_index.transpose(1, 0, 2),
        latents,
        modulation_offset,
        modulation_scale,
        modulation_gate,
        adapter_up_query_key_value[0].transpose(1, 0, 2),
        adapter_up_feedforward[0],
        adapter_down_weight[0].T,
        prior_step_cache[0],
        query_key_value_weight[0].transpose(1, 0, 2),
        feedforward_input_weight[0],
        attention_output_weight[0],
        feedforward_output_weight[0],
    )
    return record[None]


def solution(mesh):
    placed = (
        P(None, "head", None),
        P(),
        P("section", None, "head", None, None),
        P("section", None, None),
        P("section", None),
        P("section", None),
        P("section", None),
        P("section", None, None, "head"),
        P("section", None, "head"),
        P("section", None, None),
        P("section", None, None, "head"),
        P("section", None, "head"),
        P("section", "head", None),
        P("section", "head", None),
    )
    return jax.shard_map(
        per_device,
        mesh=mesh,
        in_specs=placed,
        out_specs=P("section", None, "head", None),
        check_vma=False,
    )
```

```python
import math

import jax
import jax.numpy as jnp
from jax import lax
from jax.experimental import pallas as pl
from jax.experimental.pallas import tpu as pltpu
from jax.sharding import PartitionSpec as P

DH = 128
MESH = pl.DeviceIdType.MESH
F32 = jnp.float32
BF16 = jnp.bfloat16
A, B = 0, 1

ORDER = [
    (0, 0), (1, 0), (3, 0), (2, 0), (0, 1), (0, 3), (0, 2),
    (1, 1), (1, 3), (3, 1), (3, 3), (1, 2), (3, 2), (2, 1), (2, 3), (2, 2),
]
EARLY = 7 * 16
FAR_FIRST = (2, 1, 3)
NEAR_FIRST = (1, 3, 2)


def along(axis, d):
    return (d, 0) if axis == 0 else (0, d)


def slot(place):
    return ORDER.index((place[0] % 4, place[1] % 4))


GATHER = []
for axis in (0, 1):
    GATHER += [(axis, (0, 0), along(axis, d)) for d in FAR_FIRST]
for axis in (0, 1):
    GATHER += [(1 - axis, (0, 0), along(axis, d)) for d in FAR_FIRST]
FORWARD = []
for d in NEAR_FIRST:
    for axis in (0, 1):
        first = GATHER.index((axis, (0, 0), along(axis, d)))
        after = [(axis, along(axis, -d % 4), along(1 - axis, e)) for e in FAR_FIRST]
        FORWARD.append((first, range(len(GATHER), len(GATHER) + 3)))
        GATHER += after


def rms_unit(values):
    return values * lax.rsqrt(jnp.mean(values * values, axis=-1, keepdims=True) + 1e-06)


def kernel(
    pn, bidx, lat_hbm, off_hbm, scl_hbm, gate_hbm, upq_hbm, upf_hbm, dnt_hbm, cache_hbm, wqkv_hbm,
    wffn_hbm, woa_hbm, wof_hbm,
    out,
    lat, off, scl, gate, upq, upf, dnt, next_off, next_scl, ahead,
    win, wout, cachev, skv, r1, kv, xin, xg, qkv, act, part, rb, tb, r2,
    ag_s, ag_r, rs_s, rs_r, st_s, st_r, x_s, x_r, w_sem, turn, nx_s, nm_s, nm_r,
):
    patches = xin.shape[0]
    sections = lax.axis_size("section")
    sec = lax.axis_index("section")
    head = lax.axis_index("head")
    x = head // 4
    y = lax.rem(head, 4)

    def px(d):
        return lax.rem(x + (d + 4), 4)

    def py(d):
        return lax.rem(y + (d + 4), 4)

    def dev(d):
        return (sec, px(d[0]) * 4 + py(d[1]))

    first_section = sec == 0
    even = lax.rem(sec, 2) == 0
    odd = lax.rem(sec, 2) == 1

    w_copies = [
        pltpu.make_async_copy(cache_hbm, cachev, w_sem.at[0]),
        pltpu.make_async_copy(wqkv_hbm.at[0], win.at[:, pl.ds(0, DH)], w_sem.at[1]),
        pltpu.make_async_copy(wqkv_hbm.at[1], win.at[:, pl.ds(DH, DH)], w_sem.at[2]),
        pltpu.make_async_copy(wqkv_hbm.at[2], win.at[:, pl.ds(2 * DH, DH)], w_sem.at[3]),
        pltpu.make_async_copy(wffn_hbm, win.at[:, pl.ds(3 * DH, 768)], w_sem.at[4]),
        pltpu.make_async_copy(woa_hbm, wout.at[pl.ds(0, DH)], w_sem.at[5]),
        pltpu.make_async_copy(wof_hbm, wout.at[pl.ds(DH, 768)], w_sem.at[6]),
    ]
    v_copies = [
        pltpu.make_async_copy(source, target, w_sem.at[7 + i])
        for i, (source, target) in enumerate((
            (off_hbm, off), (scl_hbm, scl), (gate_hbm, gate), (upq_hbm, upq), (upf_hbm, upf),
            (dnt_hbm, dnt), (lat_hbm, lat),
        ))
    ]

    @pl.when(first_section)
    def _():
        v_copies[6].start()

    for copy in v_copies[:3]:
        copy.start()
    w_copies[0].start()
    for copy in v_copies[3:6]:
        copy.start()

    barrier = pltpu.get_barrier_semaphore()
    for d in FAR_FIRST:
        for axis in (0, 1):
            pl.semaphore_signal(
                barrier, inc=1, device_id=dev(along(axis, d)), device_id_type=MESH
            )
    for step in (1, sections - 1):
        neighbour = (lax.rem(sec + step, sections), head)
        pl.semaphore_signal(barrier, inc=1, device_id=neighbour, device_id_type=MESH)

    @pl.when(odd)
    def _():
        for d in FAR_FIRST:
            for axis in (0, 1):
                way = along(axis, d)
                peer = (sec - 1, px(way[0]) * 4 + py(way[1]))
                pl.semaphore_signal(barrier, inc=1, device_id=peer, device_id_type=MESH)

    pl.semaphore_wait(barrier, jnp.where(even, 14, 8))

    def remote(src, dst, ssem, rsem, device):
        return pltpu.make_async_remote_copy(
            src_ref=src, dst_ref=dst, send_sem=ssem, recv_sem=rsem, device_id=device,
            device_id_type=MESH,
        )

    def gather_copy(m, i):
        hf, place, way = GATHER[i]
        there = slot((place[0] - way[0], place[1] - way[1]))
        return remote(
            xg.at[m, hf, slot(place)], xg.at[m, hf, there], ag_s.at[m, i], ag_r.at[m, i], dev(way)
        )

    def next_copy(m, i):
        if i == 12:
            return remote(
                ahead.at[m], xg.at[m, :, 0], nx_s.at[m, 12], ag_r.at[m, len(GATHER)], (sec + 1, head)
            )
        hf, _, way = GATHER[i]
        there = slot((-way[0], -way[1]))
        target = (sec + 1, px(way[0]) * 4 + py(way[1]))
        return remote(
            ahead.at[m, hf], xg.at[m, hf, there], nx_s.at[m, i], ag_r.at[m, i], target
        )

    def own_landed(m):
        ref = xg.at[m, :, 0]
        remote(ref, ref, nx_s.at[m, 12], ag_r.at[m, len(GATHER)], (sec - 1, head)).wait_recv()

    def modulation_copy(i):
        source, target = ((off, next_off), (scl, next_scl))[i]
        return remote(source, target, nm_s.at[i], nm_r.at[i], (sec - 1, head))

    def gather_landed(m, i):
        hf, place, way = GATHER[i]
        ref = xg.at[m, hf, slot((place[0] - way[0], place[1] - way[1]))]
        remote(ref, ref, ag_s.at[m, i], ag_r.at[m, i], dev((-way[0], -way[1]))).wait_recv()

    def stale_first(m, i):
        if i < 3:
            d = (1, -1, 2)[i]
            return remote(
                skv.at[m, 0, px(d)], r1.at[m, 0, x], st_s.at[m, i], st_r.at[m, i], dev((d, 0))
            )
        d = (1, -1, 2)[i - 3]
        return remote(
            skv.at[m, 1, py(d)], r1.at[m, 1, y], st_s.at[m, i], st_r.at[m, i], dev((0, d))
        )

    def stale_first_landed(m, i):
        if i < 3:
            d = (-1, 1, 2)[i]
            ref, device = r1.at[m, 0, px(d)], dev((d, 0))
        else:
            d = (-1, 1, 2)[i - 3]
            ref, device = r1.at[m, 1, py(d)], dev((0, d))
        remote(ref, ref, st_s.at[m, i], st_r.at[m, i], device).wait_recv()

    def stale_second(m, i):
        if i < 9:
            d = (1, -1, 2)[i - 6]
            return remote(
                r1.at[m, 0, :, py(d)], kv.at[m, 0, y], st_s.at[m, i], st_r.at[m, i], dev((0, d))
            )
        d = (1, -1, 2)[i - 9]
        return remote(
            r1.at[m, 1, :, px(d)], kv.at[m, 1, x], st_s.at[m, i], st_r.at[m, i], dev((d, 0))
        )

    def stale_second_landed(m, i):
        if i < 9:
            d = (-1, 1, 2)[i - 6]
            ref, device = kv.at[m, 0, py(d)], dev((0, d))
        else:
            d = (-1, 1, 2)[i - 9]
            ref, device = kv.at[m, 1, px(d)], dev((d, 0))
        remote(ref, ref, st_s.at[m, i], st_r.at[m, i], device).wait_recv()

    def stale_send(m):
        def one(j, _):
            block = bidx[m, 0, j]
            both = cachev[block]
            keys = both[:, 0].astype(F32)
            values = both[:, 1]
            rows = pl.ds(pl.multiple_of(j * 16, 16), 16)
            for h in range(16):
                part_k = keys[:, h * DH:(h + 1) * DH]
                skv[m, 0, h // 4, h % 4, rows, :] = rms_unit(part_k).astype(BF16)
                skv[m, 1, h % 4, h // 4, rows, :] = values[:, h * DH:(h + 1) * DH]
            return 0

        lax.fori_loop(0, 4, one, 0)
        for i in range(6):
            stale_first(m, i).start()
        r1[m, 0, x] = skv[m, 0, x]
        r1[m, 1, y] = skv[m, 1, y]

    def stale_forward(m):
        for i in range(3):
            stale_first_landed(m, i)
        for i in range(6, 9):
            stale_second(m, i).start()
        for i in range(3, 6):
            stale_first_landed(m, i)
        for i in range(9, 12):
            stale_second(m, i).start()
        kv[m, 0, y] = r1[m, 0, :, y]
        kv[m, 1, x] = r1[m, 1, :, x]

    def sum_way(i):
        second, c, d = i // 12, i % 12 // 3, FAR_FIRST[i % 3]
        return c, d, along((1 - c % 2) if second == 0 else c % 2, d)

    def sum_copy(m, i):
        c, d, way = sum_way(i)
        if i < 12:
            source = part.at[m, c, :, d] if c % 2 == 0 else part.at[m, c, d]
            target = rb.at[m, i]
        else:
            source, target = tb.at[m, c, d], r2.at[m, i - 12]
        return remote(source, target, rs_s.at[m, i], rs_r.at[m, i], dev(way))

    def sum_landed(m, i):
        _, _, way = sum_way(i)
        target = rb.at[m, i] if i < 12 else r2.at[m, i - 12]
        remote(
            target, target, rs_s.at[m, i], rs_r.at[m, i], dev((-way[0], -way[1]))
        ).wait_recv()

    def hand_on(m, c):
        cols = pl.ds(c * 768, 768)
        return remote(
            out.at[m, :, cols], xin.at[m, :, cols], x_s.at[m, c], x_r.at[m, c], (sec + 1, head)
        )

    def handed(m, c):
        ref = xin.at[m, :, pl.ds(c * 768, 768)]
        remote(ref, ref, x_s.at[m, c], x_r.at[m, c], (sec - 1, head)).wait_recv()

    def modulated(rows, scale, offset):
        values = rows.astype(F32)
        center = values - jnp.mean(values, axis=-1, keepdims=True)
        spread = jnp.mean(center * center, axis=-1, keepdims=True)
        normed = center * lax.rsqrt(spread + 1e-06)
        return (normed * (1.0 + scale[...]) + offset[...]).astype(BF16)

    def modulate_and_send(m):
        @pl.when(first_section)
        def _():
            xin[m] = lat[pn[m]]

        @pl.when(sec > 0)
        def _():
            for c in range(4):
                handed(m, c)

        modded = modulated(xin[m], scl, off)
        xg[m, A, 0] = modded[:, :1536]
        xg[m, B, 0] = modded[:, 1536:]
        for i in range(12):
            gather_copy(m, i).start()

    def gather_forward(m):
        for first, after in FORWARD:
            gather_landed(m, first)
            for i in after:
                gather_copy(m, i).start()
        for i in range(6, 12):
            gather_landed(m, i)

    def gather_rest(m):
        for i in range(12, len(GATHER)):
            gather_landed(m, i)

    def dot(a, b):
        return jnp.dot(a, b, preferred_element_type=F32)

    def dot_tn(a, b):
        return lax.dot_general(a, b, (((0,), (0,)), ((), ())), preferred_element_type=F32)

    def dot_nt(a, b):
        return lax.dot_general(a, b, (((1,), (1,)), ((), ())), preferred_element_type=F32)

    def merge(i, _):
        rows = pl.ds(pl.multiple_of(i * 256, 256), 256)
        down = dnt[:, rows]
        for n in range(3):
            win[rows, n * DH:(n + 1) * DH] = (
                win[rows, n * DH:(n + 1) * DH].astype(F32) + dot_tn(down, upq[n])
            ).astype(BF16)
            cols = slice(3 * DH + n * 256, 3 * DH + (n + 1) * 256)
            win[rows, cols] = (
                win[rows, cols].astype(F32) + dot_tn(down, upf[:, n * 256:(n + 1) * 256])
            ).astype(BF16)
        return 0

    def project(m, lo, hi):
        def tile(first, width):
            acc = None
            for hf in range(2):
                rows = xg[m, hf, lo // 16:hi // 16].reshape(hi - lo, 1536)
                term = dot(rows, win[hf * 1536:(hf + 1) * 1536, pl.ds(first, width)])
                acc = term if acc is None else acc + term
            return acc

        qkv[lo:hi, 0:256] = tile(0, 256)
        qkv[lo:hi, 256:384] = tile(256, DH)

        def feed(n, _):
            cols = pl.ds(pl.multiple_of(n * 256 + DH, DH), 256)
            acc = tile(pl.multiple_of(n * 256 + 3 * DH, DH), 256)
            act[lo:hi, cols] = jax.nn.gelu(acc, approximate=True).astype(BF16)
            return 0

        lax.fori_loop(0, 3, feed, 0)

    def attend_to(queries, keys, values, state):
        expo = jnp.exp(dot_nt(queries, keys) * (1.0 / math.sqrt(DH)))
        total = jnp.sum(expo, axis=-1, keepdims=True)
        mixed = dot(expo.astype(BF16), values)
        return (mixed, total) if state is None else (state[0] + mixed, state[1] + total)

    def attend_cached(m, lo, hi):
        queries = rms_unit(qkv[lo:hi, 0:DH]).astype(BF16)
        state = None
        for j in range(4):
            keys = kv[m, 0, j].reshape(256, DH)
            values = kv[m, 1, :, j].reshape(256, DH)
            state = attend_to(queries, keys, values, state)
        return queries, state

    def attend_fresh(early, late):
        keys = rms_unit(qkv[:, DH:2 * DH]).astype(BF16)
        values = qkv[:, 2 * DH:3 * DH].astype(BF16)
        for lo, hi, (queries, state) in ((0, EARLY, early), (EARLY, 256, late)):
            mixed, total = attend_to(queries, keys, values, state)
            act[lo:hi, 0:DH] = (mixed / total).astype(BF16)

    def output_products(m):
        for c in range(4):
            for n in range(3):
                lo = c * 768 + n * 256
                term = dot(act[...], wout[:, lo:lo + 256]).astype(BF16)
                for k, place in enumerate(ORDER):
                    rows = term[k * 16:(k + 1) * 16]
                    part[m, c, place[0], place[1], :, n * 256:(n + 1) * 256] = rows
            for j in range(3):
                sum_copy(m, 3 * c + j).start()

    def wide(value):
        return value.astype(F32)

    def sum_up(m):
        for c in range(4):
            total = wide(part[m, c, :, 0] if c % 2 == 0 else part[m, c, 0])
            for j in range(3):
                sum_landed(m, 3 * c + j)
                total += wide(rb[m, 3 * c + j])
            tb[m, c] = total.astype(BF16)
            for j in range(3):
                sum_copy(m, 12 + 3 * c + j).start()
        for c in range(4):
            branch = wide(part[m, c, 0, 0])
            for j in range(3):
                branch += wide(rb[m, 3 * c + j, 0])
            for j in range(3):
                sum_landed(m, 12 + 3 * c + j)
                branch += wide(r2[m, 3 * c + j])

            @pl.when(odd)
            def _():
                handed(m, c)

            cols = slice(c * 768, (c + 1) * 768)
            out[m, :, cols] = (wide(xin[m, :, cols]) + gate[:, cols] * branch).astype(BF16)

            @pl.when(jnp.logical_and(odd, sec < sections - 1))
            def _():
                hand_on(m, c).start()

        @pl.when(even)
        def _():
            @pl.when(m == 0)
            def _():
                for i in range(2):
                    source = (next_off, next_scl)[i]
                    remote(
                        source, source, nm_s.at[i], nm_r.at[i], (sec + 1, head)
                    ).wait_recv()

            modded = modulated(out[m], next_scl, next_off)
            ahead[m, A] = modded[:, :1536]
            ahead[m, B] = modded[:, 1536:]
            for i in range(13):
                next_copy(m, i).start()
            for c in range(4):
                hand_on(m, c).start()

    def stale_send_step(m, _):
        stale_send(m)
        return 0

    def stale_forward_step(m, _):
        stale_forward(m)
        return 0

    for copy in v_copies[:3]:
        copy.wait()

    @pl.when(odd)
    def _():
        for i in range(2):
            modulation_copy(i).start()

    @pl.when(sec > 0)
    def _():
        w_copies[0].wait()
        for copy in w_copies[1:]:
            copy.start()
        lax.fori_loop(0, patches, stale_send_step, 0)
        for copy in w_copies[1:5] + v_copies[3:6]:
            copy.wait()
        lax.fori_loop(0, 12, merge, 0)
        lax.fori_loop(0, patches, stale_forward_step, 0)

    @pl.when(first_section)
    def _():
        v_copies[6].wait()

    def await_turn(m):
        @pl.when(m > 0)
        def _():
            pl.semaphore_wait(turn, 1)

    def give_turn(m):
        @pl.when(jnp.logical_and(lax.rem(sec, 2) == 1, m < patches - 1))
        def _():
            pl.semaphore_signal(turn, inc=1, device_id=(sec - 1, head), device_id_type=MESH)

    def patch(m, _):
        opening = jnp.logical_and(sec == 0, m == 0)

        @pl.when(even)
        def _():
            await_turn(m)
            modulate_and_send(m)

        @pl.when(opening)
        def _():
            w_copies[0].wait()
            for copy in w_copies[1:]:
                copy.start()
            stale_send(0)

        gather_forward(m)
        give_turn(m)

        @pl.when(opening)
        def _():
            for copy in w_copies[1:5] + v_copies[3:6]:
                copy.wait()
            lax.fori_loop(0, 12, merge, 0)
            stale_forward(0)

        @pl.when(odd)
        def _():
            own_landed(m)

        project(m, 0, EARLY)
        for i in range(6, 12):
            stale_second_landed(m, i)
        early = attend_cached(m, 0, EARLY)
        gather_rest(m)
        project(m, EARLY, 256)

        @pl.when(opening)
        def _():
            lax.fori_loop(1, patches, stale_send_step, 0)

        late = attend_cached(m, EARLY, 256)
        attend_fresh(early, late)

        @pl.when(m == 0)
        def _():
            for copy in w_copies[5:]:
                copy.wait()

        output_products(m)

        @pl.when(opening)
        def _():
            lax.fori_loop(1, patches, stale_forward_step, 0)

        sum_up(m)
        return 0

    lax.fori_loop(0, patches, patch, 0)

    def drain(m, _):
        @pl.when(even)
        def _():
            for i in range(12):
                gather_copy(m, i).wait_send()
            for i in range(13):
                next_copy(m, i).wait_send()

        for i in range(12, len(GATHER)):
            gather_copy(m, i).wait_send()
        for i in range(24):
            sum_copy(m, i).wait_send()
        for i in range(6):
            stale_first(m, i).wait_send()
        for i in range(6, 12):
            stale_second(m, i).wait_send()

        @pl.when(sec < sections - 1)
        def _():
            for c in range(4):
                hand_on(m, c).wait_send()

        return 0

    lax.fori_loop(0, patches, drain, 0)

    @pl.when(odd)
    def _():
        for i in range(2):
            modulation_copy(i).wait_send()


def per_device(
    latents, patch_numbers, prior_step_cache, old_block_index, modulation_offset, modulation_scale,
    modulation_gate, query_key_value_weight, feedforward_input_weight, adapter_down_weight,
    adapter_up_query_key_value, adapter_up_feedforward, attention_output_weight,
    feedforward_output_weight,
):
    patches = old_block_index.shape[1]
    vmem = pl.BlockSpec(memory_space=pltpu.VMEM)
    smem = pl.BlockSpec(memory_space=pltpu.SMEM)
    hbm = pl.BlockSpec(memory_space=pl.ANY)
    dma = pltpu.SemaphoreType.DMA
    record = pl.pallas_call(
        kernel,
        out_shape=jax.ShapeDtypeStruct((patches, 16, 3072), BF16),
        in_specs=[smem, smem] + [hbm] * 12,
        out_specs=vmem,
        scratch_shapes=[
            pltpu.VMEM(latents.shape, BF16),
            pltpu.VMEM((1, 3072), F32),
            pltpu.VMEM((1, 3072), F32),
            pltpu.VMEM((1, 3072), F32),
            pltpu.VMEM((3, 64, DH), BF16),
            pltpu.VMEM((64, 768), BF16),
            pltpu.VMEM((64, 3072), BF16),
            pltpu.VMEM((1, 3072), F32),
            pltpu.VMEM((1, 3072), F32),
            pltpu.VMEM((patches, 2, 16, 1536), BF16),
            pltpu.VMEM((3072, 1152), BF16),
            pltpu.VMEM((896, 3072), BF16),
            pltpu.VMEM((16, 16, 2, 2048), BF16),
            pltpu.VMEM((patches, 2, 4, 4, 64, DH), BF16),
            pltpu.VMEM((patches, 2, 4, 4, 64, DH), BF16),
            pltpu.VMEM((patches, 2, 4, 4, 64, DH), BF16),
            pltpu.VMEM((patches, 16, 3072), BF16),
            pltpu.VMEM((patches, 2, 16, 16, 1536), BF16),
            pltpu.VMEM((256, 3 * DH), F32),
            pltpu.VMEM((256, 896), BF16),
            pltpu.VMEM((patches, 4, 4, 4, 16, 768), BF16),
            pltpu.VMEM((patches, 12, 4, 16, 768), BF16),
            pltpu.VMEM((patches, 4, 4, 16, 768), BF16),
            pltpu.VMEM((patches, 12, 16, 768), BF16),
            dma((patches, len(GATHER))),
            dma((patches, len(GATHER) + 1)),
            dma((patches, 24)),
            dma((patches, 24)),
            dma((patches, 12)),
            dma((patches, 12)),
            dma((patches, 4)),
            dma((patches, 4)),
            dma((14,)),
            pltpu.SemaphoreType.REGULAR,
            dma((patches, 13)),
            dma((2,)),
            dma((2,)),
        ],
        compiler_params=pltpu.CompilerParams(
            collective_id=0, has_side_effects=True, vmem_limit_bytes=58 * 2**20
        ),
        cost_estimate=pl.CostEstimate(
            flops=10_000_000_000, bytes_accessed=16_000_000, transcendentals=2_000_000
        ),
    )(
        patch_numbers,
        old_block_index.transpose(1, 0, 2),
        latents,
        modulation_offset,
        modulation_scale,
        modulation_gate,
        adapter_up_query_key_value[0].transpose(1, 0, 2),
        adapter_up_feedforward[0],
        adapter_down_weight[0].T,
        prior_step_cache[0],
        query_key_value_weight[0].transpose(1, 0, 2),
        feedforward_input_weight[0],
        attention_output_weight[0],
        feedforward_output_weight[0],
    )
    return record[None]


def solution(mesh):
    placed = (
        P(None, "head", None),
        P(),
        P("section", None, "head", None, None),
        P("section", None, None),
        P("section", None),
        P("section", None),
        P("section", None),
        P("section", None, None, "head"),
        P("section", None, "head"),
        P("section", None, None),
        P("section", None, None, "head"),
        P("section", None, "head"),
        P("section", "head", None),
        P("section", "head", None),
    )
    return jax.shard_map(
        per_device,
        mesh=mesh,
        in_specs=placed,
        out_specs=P("section", None, "head", None),
        check_vma=False,
    )
```

```python
import math

import jax
import jax.numpy as jnp
from jax import lax
from jax.experimental import pallas as pl
from jax.experimental.pallas import tpu as pltpu
from jax.sharding import PartitionSpec as P

DH = 128
MESH = pl.DeviceIdType.MESH
F32 = jnp.float32
BF16 = jnp.bfloat16
A, B = 0, 1

ORDER = [
    (0, 0), (1, 0), (3, 0), (2, 0), (0, 1), (0, 3), (0, 2),
    (1, 1), (1, 3), (3, 1), (3, 3), (1, 2), (3, 2), (2, 1), (2, 3), (2, 2),
]
EARLY = 7 * 16
FAR_FIRST = (2, 1, 3)
NEAR_FIRST = (1, 3, 2)


def along(axis, d):
    return (d, 0) if axis == 0 else (0, d)


def slot(place):
    return ORDER.index((place[0] % 4, place[1] % 4))


GATHER = []
for axis in (0, 1):
    GATHER += [(axis, (0, 0), along(axis, d)) for d in FAR_FIRST]
for axis in (0, 1):
    GATHER += [(1 - axis, (0, 0), along(axis, d)) for d in FAR_FIRST]
FORWARD = []
for d in NEAR_FIRST:
    for axis in (0, 1):
        first = GATHER.index((axis, (0, 0), along(axis, d)))
        after = [(axis, along(axis, -d % 4), along(1 - axis, e)) for e in FAR_FIRST]
        FORWARD.append((first, range(len(GATHER), len(GATHER) + 3)))
        GATHER += after


def rms_unit(values):
    return values * lax.rsqrt(jnp.mean(values * values, axis=-1, keepdims=True) + 1e-06)


def kernel(
    pn, bidx, lat_hbm, off_hbm, scl_hbm, gate_hbm, upq_hbm, upf_hbm, dnt_hbm, cache_hbm, wqkv_hbm,
    wffn_hbm, woa_hbm, wof_hbm,
    out,
    lat, off, scl, gate, upq, upf, dnt, next_off, next_scl, ahead,
    win, wout, cachev, skv, r1, kv, xin, xg, qkv, act, part, rb, tb, r2,
    ag_s, ag_r, rs_s, rs_r, st_s, st_r, x_s, x_r, w_sem, turn, nx_s, nm_s, nm_r,
):
    patches = xin.shape[0]
    sections = lax.axis_size("section")
    sec = lax.axis_index("section")
    head = lax.axis_index("head")
    x = head // 4
    y = lax.rem(head, 4)

    def px(d):
        return lax.rem(x + (d + 4), 4)

    def py(d):
        return lax.rem(y + (d + 4), 4)

    def dev(d):
        return (sec, px(d[0]) * 4 + py(d[1]))

    first_section = sec == 0
    even = lax.rem(sec, 2) == 0
    odd = lax.rem(sec, 2) == 1

    w_copies = [
        pltpu.make_async_copy(cache_hbm, cachev, w_sem.at[0]),
        pltpu.make_async_copy(wqkv_hbm.at[0], win.at[:, pl.ds(0, DH)], w_sem.at[1]),
        pltpu.make_async_copy(wqkv_hbm.at[1], win.at[:, pl.ds(DH, DH)], w_sem.at[2]),
        pltpu.make_async_copy(wqkv_hbm.at[2], win.at[:, pl.ds(2 * DH, DH)], w_sem.at[3]),
        pltpu.make_async_copy(wffn_hbm, win.at[:, pl.ds(3 * DH, 768)], w_sem.at[4]),
        pltpu.make_async_copy(woa_hbm, wout.at[pl.ds(0, DH)], w_sem.at[5]),
        pltpu.make_async_copy(wof_hbm, wout.at[pl.ds(DH, 768)], w_sem.at[6]),
    ]
    v_copies = [
        pltpu.make_async_copy(source, target, w_sem.at[7 + i])
        for i, (source, target) in enumerate((
            (off_hbm, off), (scl_hbm, scl), (gate_hbm, gate), (upq_hbm, upq), (upf_hbm, upf),
            (dnt_hbm, dnt), (lat_hbm, lat),
        ))
    ]

    @pl.when(first_section)
    def _():
        v_copies[6].start()

    for copy in v_copies[:3]:
        copy.start()
    w_copies[0].start()
    for copy in v_copies[3:6]:
        copy.start()

    barrier = pltpu.get_barrier_semaphore()
    for d in FAR_FIRST:
        for axis in (0, 1):
            pl.semaphore_signal(
                barrier, inc=1, device_id=dev(along(axis, d)), device_id_type=MESH
            )
    for step in (1, sections - 1):
        neighbour = (lax.rem(sec + step, sections), head)
        pl.semaphore_signal(barrier, inc=1, device_id=neighbour, device_id_type=MESH)

    @pl.when(odd)
    def _():
        for d in FAR_FIRST:
            for axis in (0, 1):
                way = along(axis, d)
                peer = (sec - 1, px(way[0]) * 4 + py(way[1]))
                pl.semaphore_signal(barrier, inc=1, device_id=peer, device_id_type=MESH)

    pl.semaphore_wait(barrier, jnp.where(even, 14, 8))

    def remote(src, dst, ssem, rsem, device):
        return pltpu.make_async_remote_copy(
            src_ref=src, dst_ref=dst, send_sem=ssem, recv_sem=rsem, device_id=device,
            device_id_type=MESH,
        )

    def gather_copy(m, i):
        hf, place, way = GATHER[i]
        there = slot((place[0] - way[0], place[1] - way[1]))
        return remote(
            xg.at[m, hf, slot(place)], xg.at[m, hf, there], ag_s.at[m, i], ag_r.at[m, i], dev(way)
        )

    def next_copy(m, i):
        if i == 12:
            return remote(
                ahead.at[m], xg.at[m, :, 0], nx_s.at[m, 12], ag_r.at[m, len(GATHER)], (sec + 1, head)
            )
        hf, _, way = GATHER[i]
        there = slot((-way[0], -way[1]))
        target = (sec + 1, px(way[0]) * 4 + py(way[1]))
        return remote(
            ahead.at[m, hf], xg.at[m, hf, there], nx_s.at[m, i], ag_r.at[m, i], target
        )

    def own_landed(m):
        ref = xg.at[m, :, 0]
        remote(ref, ref, nx_s.at[m, 12], ag_r.at[m, len(GATHER)], (sec - 1, head)).wait_recv()

    def modulation_copy(i):
        source, target = ((off, next_off), (scl, next_scl))[i]
        return remote(source, target, nm_s.at[i], nm_r.at[i], (sec - 1, head))

    def gather_landed(m, i):
        hf, place, way = GATHER[i]
        ref = xg.at[m, hf, slot((place[0] - way[0], place[1] - way[1]))]
        remote(ref, ref, ag_s.at[m, i], ag_r.at[m, i], dev((-way[0], -way[1]))).wait_recv()

    def stale_first(m, i):
        if i < 3:
            d = (1, -1, 2)[i]
            return remote(
                skv.at[m, 0, px(d)], r1.at[m, 0, x], st_s.at[m, i], st_r.at[m, i], dev((d, 0))
            )
        d = (1, -1, 2)[i - 3]
        return remote(
            skv.at[m, 1, py(d)], r1.at[m, 1, y], st_s.at[m, i], st_r.at[m, i], dev((0, d))
        )

    def stale_first_landed(m, i):
        if i < 3:
            d = (-1, 1, 2)[i]
            ref, device = r1.at[m, 0, px(d)], dev((d, 0))
        else:
            d = (-1, 1, 2)[i - 3]
            ref, device = r1.at[m, 1, py(d)], dev((0, d))
        remote(ref, ref, st_s.at[m, i], st_r.at[m, i], device).wait_recv()

    def stale_second(m, i):
        if i < 9:
            d = (1, -1, 2)[i - 6]
            return remote(
                r1.at[m, 0, :, py(d)], kv.at[m, 0, y], st_s.at[m, i], st_r.at[m, i], dev((0, d))
            )
        d = (1, -1, 2)[i - 9]
        return remote(
            r1.at[m, 1, :, px(d)], kv.at[m, 1, x], st_s.at[m, i], st_r.at[m, i], dev((d, 0))
        )

    def stale_second_landed(m, i):
        if i < 9:
            d = (-1, 1, 2)[i - 6]
            ref, device = kv.at[m, 0, py(d)], dev((0, d))
        else:
            d = (-1, 1, 2)[i - 9]
            ref, device = kv.at[m, 1, px(d)], dev((d, 0))
        remote(ref, ref, st_s.at[m, i], st_r.at[m, i], device).wait_recv()

    def stale_send(m):
        def one(j, _):
            block = bidx[m, 0, j]
            both = cachev[block]
            keys = both[:, 0].astype(F32)
            values = both[:, 1]
            rows = pl.ds(pl.multiple_of(j * 16, 16), 16)
            for h in range(16):
                part_k = keys[:, h * DH:(h + 1) * DH]
                skv[m, 0, h // 4, h % 4, rows, :] = rms_unit(part_k).astype(BF16)
                skv[m, 1, h % 4, h // 4, rows, :] = values[:, h * DH:(h + 1) * DH]
            return 0

        lax.fori_loop(0, 4, one, 0)
        for i in range(6):
            stale_first(m, i).start()
        r1[m, 0, x] = skv[m, 0, x]
        r1[m, 1, y] = skv[m, 1, y]

    def stale_forward(m):
        for i in range(3):
            stale_first_landed(m, i)
        for i in range(6, 9):
            stale_second(m, i).start()
        for i in range(3, 6):
            stale_first_landed(m, i)
        for i in range(9, 12):
            stale_second(m, i).start()
        kv[m, 0, y] = r1[m, 0, :, y]
        kv[m, 1, x] = r1[m, 1, :, x]

    def sum_way(i):
        second, c, d = i // 12, i % 12 // 3, FAR_FIRST[i % 3]
        return c, d, along((1 - c % 2) if second == 0 else c % 2, d)

    def sum_copy(m, i):
        c, d, way = sum_way(i)
        if i < 12:
            source = part.at[m, c, :, d] if c % 2 == 0 else part.at[m, c, d]
            target = rb.at[m, i]
        else:
            source, target = tb.at[m, c, d], r2.at[m, i - 12]
        return remote(source, target, rs_s.at[m, i], rs_r.at[m, i], dev(way))

    def sum_landed(m, i):
        _, _, way = sum_way(i)
        target = rb.at[m, i] if i < 12 else r2.at[m, i - 12]
        remote(
            target, target, rs_s.at[m, i], rs_r.at[m, i], dev((-way[0], -way[1]))
        ).wait_recv()

    def hand_on(m, c):
        cols = pl.ds(c * 768, 768)
        return remote(
            out.at[m, :, cols], xin.at[m, :, cols], x_s.at[m, c], x_r.at[m, c], (sec + 1, head)
        )

    def handed(m, c):
        ref = xin.at[m, :, pl.ds(c * 768, 768)]
        remote(ref, ref, x_s.at[m, c], x_r.at[m, c], (sec - 1, head)).wait_recv()

    def modulated(rows, scale, offset):
        values = rows.astype(F32)
        center = values - jnp.mean(values, axis=-1, keepdims=True)
        spread = jnp.mean(center * center, axis=-1, keepdims=True)
        normed = center * lax.rsqrt(spread + 1e-06)
        return (normed * (1.0 + scale[...]) + offset[...]).astype(BF16)

    def modulate_and_send(m):
        @pl.when(first_section)
        def _():
            xin[m] = lat[pn[m]]

        @pl.when(sec > 0)
        def _():
            for c in range(4):
                handed(m, c)

        modded = modulated(xin[m], scl, off)
        xg[m, A, 0] = modded[:, :1536]
        xg[m, B, 0] = modded[:, 1536:]
        for i in range(12):
            gather_copy(m, i).start()

    def gather_forward(m):
        for first, after in FORWARD:
            gather_landed(m, first)
            for i in after:
                gather_copy(m, i).start()
        for i in range(6, 12):
            gather_landed(m, i)

    def gather_rest(m):
        for i in range(12, len(GATHER)):
            gather_landed(m, i)

    def dot(a, b):
        return jnp.dot(a, b, preferred_element_type=F32)

    def dot_tn(a, b):
        return lax.dot_general(a, b, (((0,), (0,)), ((), ())), preferred_element_type=F32)

    def dot_nt(a, b):
        return lax.dot_general(a, b, (((1,), (1,)), ((), ())), preferred_element_type=F32)

    def merge(i, _):
        rows = pl.ds(pl.multiple_of(i * 256, 256), 256)
        down = dnt[:, rows]
        for n in range(3):
            win[rows, n * DH:(n + 1) * DH] = (
                win[rows, n * DH:(n + 1) * DH].astype(F32) + dot_tn(down, upq[n])
            ).astype(BF16)
            cols = slice(3 * DH + n * 256, 3 * DH + (n + 1) * 256)
            win[rows, cols] = (
                win[rows, cols].astype(F32) + dot_tn(down, upf[:, n * 256:(n + 1) * 256])
            ).astype(BF16)
        return 0

    def project(m, lo, hi):
        def tile(first, width):
            acc = None
            for hf in range(2):
                rows = xg[m, hf, lo // 16:hi // 16].reshape(hi - lo, 1536)
                term = dot(rows, win[hf * 1536:(hf + 1) * 1536, pl.ds(first, width)])
                acc = term if acc is None else acc + term
            return acc

        qkv[lo:hi, 0:256] = tile(0, 256)
        qkv[lo:hi, 256:384] = tile(256, DH)

        def feed():
            for n in range(3):
                acc = tile(n * 256 + 3 * DH, 256)
                cols = slice(n * 256 + DH, (n + 1) * 256 + DH)
                act[lo:hi, cols] = jax.nn.gelu(acc, approximate=True).astype(BF16)

        return feed

    def attend_to(queries, keys, values, state):
        expo = jnp.exp(dot_nt(queries, keys) * (1.0 / math.sqrt(DH)))
        total = jnp.sum(expo, axis=-1, keepdims=True)
        mixed = dot(expo.astype(BF16), values)
        return (mixed, total) if state is None else (state[0] + mixed, state[1] + total)

    def attend_cached(m, lo, hi):
        queries = rms_unit(qkv[lo:hi, 0:DH]).astype(BF16)
        state = None
        for j in range(4):
            keys = kv[m, 0, j].reshape(256, DH)
            values = kv[m, 1, :, j].reshape(256, DH)
            state = attend_to(queries, keys, values, state)
        return queries, state

    def attend_fresh(early, late):
        keys = rms_unit(qkv[:, DH:2 * DH]).astype(BF16)
        values = qkv[:, 2 * DH:3 * DH].astype(BF16)
        for lo, hi, (queries, state) in ((0, EARLY, early), (EARLY, 256, late)):
            mixed, total = attend_to(queries, keys, values, state)
            act[lo:hi, 0:DH] = (mixed / total).astype(BF16)

    def output_products(m):
        for c in range(4):
            for n in range(3):
                lo = c * 768 + n * 256
                term = dot(act[...], wout[:, lo:lo + 256]).astype(BF16)
                for k, place in enumerate(ORDER):
                    rows = term[k * 16:(k + 1) * 16]
                    part[m, c, place[0], place[1], :, n * 256:(n + 1) * 256] = rows
            for j in range(3):
                sum_copy(m, 3 * c + j).start()

    def wide(value):
        return value.astype(F32)

    def sum_up(m):
        for c in range(4):
            total = wide(part[m, c, :, 0] if c % 2 == 0 else part[m, c, 0])
            for j in range(3):
                sum_landed(m, 3 * c + j)
                total += wide(rb[m, 3 * c + j])
            tb[m, c] = total.astype(BF16)
            for j in range(3):
                sum_copy(m, 12 + 3 * c + j).start()
        for c in range(4):
            branch = wide(part[m, c, 0, 0])
            for j in range(3):
                branch += wide(rb[m, 3 * c + j, 0])
            for j in range(3):
                sum_landed(m, 12 + 3 * c + j)
                branch += wide(r2[m, 3 * c + j])

            @pl.when(odd)
            def _():
                handed(m, c)

            cols = slice(c * 768, (c + 1) * 768)
            out[m, :, cols] = (wide(xin[m, :, cols]) + gate[:, cols] * branch).astype(BF16)

            @pl.when(jnp.logical_and(odd, sec < sections - 1))
            def _():
                hand_on(m, c).start()

        @pl.when(even)
        def _():
            @pl.when(m == 0)
            def _():
                for i in range(2):
                    source = (next_off, next_scl)[i]
                    remote(
                        source, source, nm_s.at[i], nm_r.at[i], (sec + 1, head)
                    ).wait_recv()

            modded = modulated(out[m], next_scl, next_off)
            ahead[m, A] = modded[:, :1536]
            ahead[m, B] = modded[:, 1536:]
            for i in range(13):
                next_copy(m, i).start()
            for c in range(4):
                hand_on(m, c).start()

    def stale_send_step(m, _):
        stale_send(m)
        return 0

    def stale_forward_step(m, _):
        stale_forward(m)
        return 0

    for copy in v_copies[:3]:
        copy.wait()

    @pl.when(odd)
    def _():
        for i in range(2):
            modulation_copy(i).start()

    @pl.when(sec > 0)
    def _():
        w_copies[0].wait()
        for copy in w_copies[1:]:
            copy.start()
        lax.fori_loop(0, patches, stale_send_step, 0)
        for copy in w_copies[1:5] + v_copies[3:6]:
            copy.wait()
        lax.fori_loop(0, 12, merge, 0)
        lax.fori_loop(0, patches, stale_forward_step, 0)

    @pl.when(first_section)
    def _():
        v_copies[6].wait()

    def await_turn(m):
        @pl.when(m > 0)
        def _():
            pl.semaphore_wait(turn, 1)

    def give_turn(m):
        @pl.when(jnp.logical_and(lax.rem(sec, 2) == 1, m < patches - 1))
        def _():
            pl.semaphore_signal(turn, inc=1, device_id=(sec - 1, head), device_id_type=MESH)

    def patch(m, _):
        opening = jnp.logical_and(sec == 0, m == 0)

        @pl.when(even)
        def _():
            await_turn(m)
            modulate_and_send(m)

        @pl.when(opening)
        def _():
            w_copies[0].wait()
            for copy in w_copies[1:]:
                copy.start()
            stale_send(0)

        gather_forward(m)
        give_turn(m)

        @pl.when(opening)
        def _():
            for copy in w_copies[1:5] + v_copies[3:6]:
                copy.wait()
            lax.fori_loop(0, 12, merge, 0)
            stale_forward(0)

        @pl.when(odd)
        def _():
            own_landed(m)

        project(m, 0, EARLY)()
        for i in range(6, 12):
            stale_second_landed(m, i)
        early = attend_cached(m, 0, EARLY)
        gather_rest(m)

        @pl.when(opening)
        def _():
            lax.fori_loop(1, patches, stale_send_step, 0)

        feed = project(m, EARLY, 256)
        late = attend_cached(m, EARLY, 256)
        feed()
        attend_fresh(early, late)

        @pl.when(m == 0)
        def _():
            for copy in w_copies[5:]:
                copy.wait()

        output_products(m)

        @pl.when(opening)
        def _():
            lax.fori_loop(1, patches, stale_forward_step, 0)

        sum_up(m)
        return 0

    lax.fori_loop(0, patches, patch, 0)

    def drain(m, _):
        @pl.when(even)
        def _():
            for i in range(12):
                gather_copy(m, i).wait_send()
            for i in range(13):
                next_copy(m, i).wait_send()

        for i in range(12, len(GATHER)):
            gather_copy(m, i).wait_send()
        for i in range(24):
            sum_copy(m, i).wait_send()
        for i in range(6):
            stale_first(m, i).wait_send()
        for i in range(6, 12):
            stale_second(m, i).wait_send()

        @pl.when(sec < sections - 1)
        def _():
            for c in range(4):
                hand_on(m, c).wait_send()

        return 0

    lax.fori_loop(0, patches, drain, 0)

    @pl.when(odd)
    def _():
        for i in range(2):
            modulation_copy(i).wait_send()


def per_device(
    latents, patch_numbers, prior_step_cache, old_block_index, modulation_offset, modulation_scale,
    modulation_gate, query_key_value_weight, feedforward_input_weight, adapter_down_weight,
    adapter_up_query_key_value, adapter_up_feedforward, attention_output_weight,
    feedforward_output_weight,
):
    patches = old_block_index.shape[1]
    vmem = pl.BlockSpec(memory_space=pltpu.VMEM)
    smem = pl.BlockSpec(memory_space=pltpu.SMEM)
    hbm = pl.BlockSpec(memory_space=pl.ANY)
    dma = pltpu.SemaphoreType.DMA
    record = pl.pallas_call(
        kernel,
        out_shape=jax.ShapeDtypeStruct((patches, 16, 3072), BF16),
        in_specs=[smem, smem] + [hbm] * 12,
        out_specs=vmem,
        scratch_shapes=[
            pltpu.VMEM(latents.shape, BF16),
            pltpu.VMEM((1, 3072), F32),
            pltpu.VMEM((1, 3072), F32),
            pltpu.VMEM((1, 3072), F32),
            pltpu.VMEM((3, 64, DH), BF16),
            pltpu.VMEM((64, 768), BF16),
            pltpu.VMEM((64, 3072), BF16),
            pltpu.VMEM((1, 3072), F32),
            pltpu.VMEM((1, 3072), F32),
            pltpu.VMEM((patches, 2, 16, 1536), BF16),
            pltpu.VMEM((3072, 1152), BF16),
            pltpu.VMEM((896, 3072), BF16),
            pltpu.VMEM((16, 16, 2, 2048), BF16),
            pltpu.VMEM((patches, 2, 4, 4, 64, DH), BF16),
            pltpu.VMEM((patches, 2, 4, 4, 64, DH), BF16),
            pltpu.VMEM((patches, 2, 4, 4, 64, DH), BF16),
            pltpu.VMEM((patches, 16, 3072), BF16),
            pltpu.VMEM((patches, 2, 16, 16, 1536), BF16),
            pltpu.VMEM((256, 3 * DH), F32),
            pltpu.VMEM((256, 896), BF16),
            pltpu.VMEM((patches, 4, 4, 4, 16, 768), BF16),
            pltpu.VMEM((patches, 12, 4, 16, 768), BF16),
            pltpu.VMEM((patches, 4, 4, 16, 768), BF16),
            pltpu.VMEM((patches, 12, 16, 768), BF16),
            dma((patches, len(GATHER))),
            dma((patches, len(GATHER) + 1)),
            dma((patches, 24)),
            dma((patches, 24)),
            dma((patches, 12)),
            dma((patches, 12)),
            dma((patches, 4)),
            dma((patches, 4)),
            dma((14,)),
            pltpu.SemaphoreType.REGULAR,
            dma((patches, 13)),
            dma((2,)),
            dma((2,)),
        ],
        compiler_params=pltpu.CompilerParams(
            collective_id=0, has_side_effects=True, vmem_limit_bytes=58 * 2**20
        ),
        cost_estimate=pl.CostEstimate(
            flops=10_000_000_000, bytes_accessed=16_000_000, transcendentals=2_000_000
        ),
    )(
        patch_numbers,
        old_block_index.transpose(1, 0, 2),
        latents,
        modulation_offset,
        modulation_scale,
        modulation_gate,
        adapter_up_query_key_value[0].transpose(1, 0, 2),
        adapter_up_feedforward[0],
        adapter_down_weight[0].T,
        prior_step_cache[0],
        query_key_value_weight[0].transpose(1, 0, 2),
        feedforward_input_weight[0],
        attention_output_weight[0],
        feedforward_output_weight[0],
    )
    return record[None]


def solution(mesh):
    placed = (
        P(None, "head", None),
        P(),
        P("section", None, "head", None, None),
        P("section", None, None),
        P("section", None),
        P("section", None),
        P("section", None),
        P("section", None, None, "head"),
        P("section", None, "head"),
        P("section", None, None),
        P("section", None, None, "head"),
        P("section", None, "head"),
        P("section", "head", None),
        P("section", "head", None),
    )
    return jax.shard_map(
        per_device,
        mesh=mesh,
        in_specs=placed,
        out_specs=P("section", None, "head", None),
        check_vma=False,
    )
```

```python
import math

import jax
import jax.numpy as jnp
from jax import lax
from jax.experimental import pallas as pl
from jax.experimental.pallas import tpu as pltpu
from jax.sharding import PartitionSpec as P

DH = 128
MESH = pl.DeviceIdType.MESH
F32 = jnp.float32
BF16 = jnp.bfloat16
A, B = 0, 1

ORDER = [
    (0, 0), (1, 0), (3, 0), (2, 0), (0, 1), (0, 3), (0, 2),
    (1, 1), (1, 3), (3, 1), (3, 3), (1, 2), (3, 2), (2, 1), (2, 3), (2, 2),
]
EARLY = 7 * 16
FAR_FIRST = (2, 1, 3)
NEAR_FIRST = (1, 3, 2)


def along(axis, d):
    return (d, 0) if axis == 0 else (0, d)


def slot(place):
    return ORDER.index((place[0] % 4, place[1] % 4))


GATHER = []
for axis in (0, 1):
    GATHER += [(axis, (0, 0), along(axis, d)) for d in FAR_FIRST]
for axis in (0, 1):
    GATHER += [(1 - axis, (0, 0), along(axis, d)) for d in FAR_FIRST]
FORWARD = []
for d in NEAR_FIRST:
    for axis in (0, 1):
        first = GATHER.index((axis, (0, 0), along(axis, d)))
        after = [(axis, along(axis, -d % 4), along(1 - axis, e)) for e in FAR_FIRST]
        FORWARD.append((first, range(len(GATHER), len(GATHER) + 3)))
        GATHER += after


def rms_unit(values):
    return values * lax.rsqrt(jnp.mean(values * values, axis=-1, keepdims=True) + 1e-06)


def kernel(
    pn, bidx, lat_hbm, off_hbm, scl_hbm, gate_hbm, upq_hbm, upf_hbm, dnt_hbm, cache_hbm, wqkv_hbm,
    wffn_hbm, woa_hbm, wof_hbm,
    out,
    lat, off, scl, gate, upq, upf, dnt, next_off, next_scl, ahead,
    win, wout, cachev, skv, r1, kv, xin, xg, qkv, act, part, rb, tb, r2,
    ag_s, ag_r, rs_s, rs_r, st_s, st_r, x_s, x_r, w_sem, turn, nx_s, nm_s, nm_r,
):
    patches = xin.shape[0]
    sections = lax.axis_size("section")
    sec = lax.axis_index("section")
    head = lax.axis_index("head")
    x = head // 4
    y = lax.rem(head, 4)

    def px(d):
        return lax.rem(x + (d + 4), 4)

    def py(d):
        return lax.rem(y + (d + 4), 4)

    def dev(d):
        return (sec, px(d[0]) * 4 + py(d[1]))

    first_section = sec == 0
    even = lax.rem(sec, 2) == 0
    odd = lax.rem(sec, 2) == 1

    w_copies = [
        pltpu.make_async_copy(cache_hbm, cachev, w_sem.at[0]),
        pltpu.make_async_copy(wqkv_hbm.at[0], win.at[:, pl.ds(0, DH)], w_sem.at[1]),
        pltpu.make_async_copy(wqkv_hbm.at[1], win.at[:, pl.ds(DH, DH)], w_sem.at[2]),
        pltpu.make_async_copy(wqkv_hbm.at[2], win.at[:, pl.ds(2 * DH, DH)], w_sem.at[3]),
        pltpu.make_async_copy(wffn_hbm, win.at[:, pl.ds(3 * DH, 768)], w_sem.at[4]),
        pltpu.make_async_copy(woa_hbm, wout.at[pl.ds(0, DH)], w_sem.at[5]),
        pltpu.make_async_copy(wof_hbm, wout.at[pl.ds(DH, 768)], w_sem.at[6]),
    ]
    v_copies = [
        pltpu.make_async_copy(source, target, w_sem.at[7 + i])
        for i, (source, target) in enumerate((
            (off_hbm, off), (scl_hbm, scl), (gate_hbm, gate), (upq_hbm, upq), (upf_hbm, upf),
            (dnt_hbm, dnt), (lat_hbm, lat),
        ))
    ]

    @pl.when(first_section)
    def _():
        v_copies[6].start()

    for copy in v_copies[:3]:
        copy.start()
    w_copies[0].start()
    for copy in v_copies[3:6]:
        copy.start()

    barrier = pltpu.get_barrier_semaphore()
    for d in FAR_FIRST:
        for axis in (0, 1):
            pl.semaphore_signal(
                barrier, inc=1, device_id=dev(along(axis, d)), device_id_type=MESH
            )
    for step in (1, sections - 1):
        neighbour = (lax.rem(sec + step, sections), head)
        pl.semaphore_signal(barrier, inc=1, device_id=neighbour, device_id_type=MESH)

    @pl.when(odd)
    def _():
        for d in FAR_FIRST:
            for axis in (0, 1):
                way = along(axis, d)
                peer = (sec - 1, px(way[0]) * 4 + py(way[1]))
                pl.semaphore_signal(barrier, inc=1, device_id=peer, device_id_type=MESH)

    pl.semaphore_wait(barrier, jnp.where(even, 14, 8))

    def remote(src, dst, ssem, rsem, device):
        return pltpu.make_async_remote_copy(
            src_ref=src, dst_ref=dst, send_sem=ssem, recv_sem=rsem, device_id=device,
            device_id_type=MESH,
        )

    def gather_copy(m, i):
        hf, place, way = GATHER[i]
        there = slot((place[0] - way[0], place[1] - way[1]))
        return remote(
            xg.at[m, hf, slot(place)], xg.at[m, hf, there], ag_s.at[m, i], ag_r.at[m, i], dev(way)
        )

    def next_copy(m, i):
        if i == 12:
            return remote(
                ahead.at[m], xg.at[m, :, 0], nx_s.at[m, 12], ag_r.at[m, len(GATHER)], (sec + 1, head)
            )
        hf, _, way = GATHER[i]
        there = slot((-way[0], -way[1]))
        target = (sec + 1, px(way[0]) * 4 + py(way[1]))
        return remote(
            ahead.at[m, hf], xg.at[m, hf, there], nx_s.at[m, i], ag_r.at[m, i], target
        )

    def own_landed(m):
        ref = xg.at[m, :, 0]
        remote(ref, ref, nx_s.at[m, 12], ag_r.at[m, len(GATHER)], (sec - 1, head)).wait_recv()

    def modulation_copy(i):
        source, target = ((off, next_off), (scl, next_scl))[i]
        return remote(source, target, nm_s.at[i], nm_r.at[i], (sec - 1, head))

    def gather_landed(m, i):
        hf, place, way = GATHER[i]
        ref = xg.at[m, hf, slot((place[0] - way[0], place[1] - way[1]))]
        remote(ref, ref, ag_s.at[m, i], ag_r.at[m, i], dev((-way[0], -way[1]))).wait_recv()

    def stale_first(m, i):
        if i < 3:
            d = (1, -1, 2)[i]
            return remote(
                skv.at[m, 0, px(d)], r1.at[m, 0, x], st_s.at[m, i], st_r.at[m, i], dev((d, 0))
            )
        d = (1, -1, 2)[i - 3]
        return remote(
            skv.at[m, 1, py(d)], r1.at[m, 1, y], st_s.at[m, i], st_r.at[m, i], dev((0, d))
        )

    def stale_first_landed(m, i):
        if i < 3:
            d = (-1, 1, 2)[i]
            ref, device = r1.at[m, 0, px(d)], dev((d, 0))
        else:
            d = (-1, 1, 2)[i - 3]
            ref, device = r1.at[m, 1, py(d)], dev((0, d))
        remote(ref, ref, st_s.at[m, i], st_r.at[m, i], device).wait_recv()

    def stale_second(m, i):
        if i < 9:
            d = (1, -1, 2)[i - 6]
            return remote(
                r1.at[m, 0, :, py(d)], kv.at[m, 0, y], st_s.at[m, i], st_r.at[m, i], dev((0, d))
            )
        d = (1, -1, 2)[i - 9]
        return remote(
            r1.at[m, 1, :, px(d)], kv.at[m, 1, x], st_s.at[m, i], st_r.at[m, i], dev((d, 0))
        )

    def stale_second_landed(m, i):
        if i < 9:
            d = (-1, 1, 2)[i - 6]
            ref, device = kv.at[m, 0, py(d)], dev((0, d))
        else:
            d = (-1, 1, 2)[i - 9]
            ref, device = kv.at[m, 1, px(d)], dev((d, 0))
        remote(ref, ref, st_s.at[m, i], st_r.at[m, i], device).wait_recv()

    def stale_send(m):
        def one(j, _):
            block = bidx[m, 0, j]
            both = cachev[block]
            keys = both[:, 0].astype(F32)
            values = both[:, 1]
            rows = pl.ds(pl.multiple_of(j * 16, 16), 16)
            for h in range(16):
                part_k = keys[:, h * DH:(h + 1) * DH]
                skv[m, 0, h // 4, h % 4, rows, :] = rms_unit(part_k).astype(BF16)
                skv[m, 1, h % 4, h // 4, rows, :] = values[:, h * DH:(h + 1) * DH]
            return 0

        lax.fori_loop(0, 4, one, 0)
        for i in range(6):
            stale_first(m, i).start()
        r1[m, 0, x] = skv[m, 0, x]
        r1[m, 1, y] = skv[m, 1, y]

    def stale_forward(m):
        for i in range(3):
            stale_first_landed(m, i)
        for i in range(6, 9):
            stale_second(m, i).start()
        for i in range(3, 6):
            stale_first_landed(m, i)
        for i in range(9, 12):
            stale_second(m, i).start()
        kv[m, 0, y] = r1[m, 0, :, y]
        kv[m, 1, x] = r1[m, 1, :, x]

    def sum_way(i):
        second, c, d = i // 12, i % 12 // 3, FAR_FIRST[i % 3]
        return c, d, along((1 - c % 2) if second == 0 else c % 2, d)

    def sum_copy(m, i):
        c, d, way = sum_way(i)
        if i < 12:
            source = part.at[m, c, :, d] if c % 2 == 0 else part.at[m, c, d]
            target = rb.at[m, i]
        else:
            source, target = tb.at[m, c, d], r2.at[m, i - 12]
        return remote(source, target, rs_s.at[m, i], rs_r.at[m, i], dev(way))

    def sum_landed(m, i):
        _, _, way = sum_way(i)
        target = rb.at[m, i] if i < 12 else r2.at[m, i - 12]
        remote(
            target, target, rs_s.at[m, i], rs_r.at[m, i], dev((-way[0], -way[1]))
        ).wait_recv()

    def hand_on(m, c):
        cols = pl.ds(c * 768, 768)
        return remote(
            out.at[m, :, cols], xin.at[m, :, cols], x_s.at[m, c], x_r.at[m, c], (sec + 1, head)
        )

    def handed(m, c):
        ref = xin.at[m, :, pl.ds(c * 768, 768)]
        remote(ref, ref, x_s.at[m, c], x_r.at[m, c], (sec - 1, head)).wait_recv()

    def modulated(rows, scale, offset):
        values = rows.astype(F32)
        center = values - jnp.mean(values, axis=-1, keepdims=True)
        spread = jnp.mean(center * center, axis=-1, keepdims=True)
        normed = center * lax.rsqrt(spread + 1e-06)
        return (normed * (1.0 + scale[...]) + offset[...]).astype(BF16)

    def modulate_and_send(m):
        @pl.when(first_section)
        def _():
            xin[m] = lat[pn[m]]

        @pl.when(sec > 0)
        def _():
            for c in range(4):
                handed(m, c)

        modded = modulated(xin[m], scl, off)
        xg[m, A, 0] = modded[:, :1536]
        xg[m, B, 0] = modded[:, 1536:]
        for i in range(12):
            gather_copy(m, i).start()

    def gather_forward(m):
        for k, (first, after) in enumerate(FORWARD):
            gather_landed(m, first)
            if k == 5:
                give_turn(m)
            for i in after:
                gather_copy(m, i).start()
        for i in range(6, 12):
            gather_landed(m, i)

    def gather_rest(m):
        for i in range(12, len(GATHER)):
            gather_landed(m, i)

    def dot(a, b):
        return jnp.dot(a, b, preferred_element_type=F32)

    def dot_tn(a, b):
        return lax.dot_general(a, b, (((0,), (0,)), ((), ())), preferred_element_type=F32)

    def dot_nt(a, b):
        return lax.dot_general(a, b, (((1,), (1,)), ((), ())), preferred_element_type=F32)

    def merge(i, _):
        rows = pl.ds(pl.multiple_of(i * 256, 256), 256)
        down = dnt[:, rows]
        for n in range(3):
            win[rows, n * DH:(n + 1) * DH] = (
                win[rows, n * DH:(n + 1) * DH].astype(F32) + dot_tn(down, upq[n])
            ).astype(BF16)
            cols = slice(3 * DH + n * 256, 3 * DH + (n + 1) * 256)
            win[rows, cols] = (
                win[rows, cols].astype(F32) + dot_tn(down, upf[:, n * 256:(n + 1) * 256])
            ).astype(BF16)
        return 0

    def project(m, lo, hi):
        def tile(first, width):
            acc = None
            for hf in range(2):
                rows = xg[m, hf, lo // 16:hi // 16].reshape(hi - lo, 1536)
                term = dot(rows, win[hf * 1536:(hf + 1) * 1536, pl.ds(first, width)])
                acc = term if acc is None else acc + term
            return acc

        qkv[lo:hi, 0:256] = tile(0, 256)
        qkv[lo:hi, 256:384] = tile(256, DH)

        def feed():
            for n in range(3):
                acc = tile(n * 256 + 3 * DH, 256)
                cols = slice(n * 256 + DH, (n + 1) * 256 + DH)
                act[lo:hi, cols] = jax.nn.gelu(acc, approximate=True).astype(BF16)

        return feed

    def attend_to(queries, keys, values, state):
        expo = jnp.exp(dot_nt(queries, keys) * (1.0 / math.sqrt(DH)))
        total = jnp.sum(expo, axis=-1, keepdims=True)
        mixed = dot(expo.astype(BF16), values)
        return (mixed, total) if state is None else (state[0] + mixed, state[1] + total)

    def attend_cached(m, lo, hi):
        queries = rms_unit(qkv[lo:hi, 0:DH]).astype(BF16)
        state = None
        for j in range(4):
            keys = kv[m, 0, j].reshape(256, DH)
            values = kv[m, 1, :, j].reshape(256, DH)
            state = attend_to(queries, keys, values, state)
        return queries, state

    def attend_fresh(early, late):
        keys = rms_unit(qkv[:, DH:2 * DH]).astype(BF16)
        values = qkv[:, 2 * DH:3 * DH].astype(BF16)
        for lo, hi, (queries, state) in ((0, EARLY, early), (EARLY, 256, late)):
            mixed, total = attend_to(queries, keys, values, state)
            act[lo:hi, 0:DH] = (mixed / total).astype(BF16)

    def output_products(m):
        for c in range(4):
            for n in range(3):
                lo = c * 768 + n * 256
                term = dot(act[...], wout[:, lo:lo + 256]).astype(BF16)
                for k, place in enumerate(ORDER):
                    rows = term[k * 16:(k + 1) * 16]
                    part[m, c, place[0], place[1], :, n * 256:(n + 1) * 256] = rows
            for j in range(3):
                sum_copy(m, 3 * c + j).start()

    def wide(value):
        return value.astype(F32)

    def sum_up(m):
        for c in range(4):
            total = wide(part[m, c, :, 0] if c % 2 == 0 else part[m, c, 0])
            for j in range(3):
                sum_landed(m, 3 * c + j)
                total += wide(rb[m, 3 * c + j])
            tb[m, c] = total.astype(BF16)
            for j in range(3):
                sum_copy(m, 12 + 3 * c + j).start()
        for c in range(4):
            branch = wide(part[m, c, 0, 0])
            for j in range(3):
                branch += wide(rb[m, 3 * c + j, 0])
            for j in range(3):
                sum_landed(m, 12 + 3 * c + j)
                branch += wide(r2[m, 3 * c + j])

            @pl.when(odd)
            def _():
                handed(m, c)

            cols = slice(c * 768, (c + 1) * 768)
            out[m, :, cols] = (wide(xin[m, :, cols]) + gate[:, cols] * branch).astype(BF16)

            @pl.when(jnp.logical_and(odd, sec < sections - 1))
            def _():
                hand_on(m, c).start()

        @pl.when(even)
        def _():
            @pl.when(m == 0)
            def _():
                for i in range(2):
                    source = (next_off, next_scl)[i]
                    remote(
                        source, source, nm_s.at[i], nm_r.at[i], (sec + 1, head)
                    ).wait_recv()

            modded = modulated(out[m], next_scl, next_off)
            ahead[m, A] = modded[:, :1536]
            ahead[m, B] = modded[:, 1536:]
            for i in range(13):
                next_copy(m, i).start()
            for c in range(4):
                hand_on(m, c).start()

    def stale_send_step(m, _):
        stale_send(m)
        return 0

    def stale_forward_step(m, _):
        stale_forward(m)
        return 0

    for copy in v_copies[:3]:
        copy.wait()

    @pl.when(odd)
    def _():
        for i in range(2):
            modulation_copy(i).start()

    @pl.when(sec > 0)
    def _():
        w_copies[0].wait()
        for copy in w_copies[1:]:
            copy.start()
        lax.fori_loop(0, patches, stale_send_step, 0)
        for copy in w_copies[1:5] + v_copies[3:6]:
            copy.wait()
        lax.fori_loop(0, 12, merge, 0)
        lax.fori_loop(0, patches, stale_forward_step, 0)

    @pl.when(first_section)
    def _():
        v_copies[6].wait()

    def await_turn(m):
        @pl.when(m > 0)
        def _():
            pl.semaphore_wait(turn, 1)

    def give_turn(m):
        @pl.when(jnp.logical_and(lax.rem(sec, 2) == 1, m < patches - 1))
        def _():
            pl.semaphore_signal(turn, inc=1, device_id=(sec - 1, head), device_id_type=MESH)

    def drain_early(m):
        @pl.when(even)
        def _():
            for i in range(12):
                gather_copy(m, i).wait_send()

        for i in range(12, len(GATHER)):
            gather_copy(m, i).wait_send()
        for i in range(6):
            stale_first(m, i).wait_send()
        for i in range(6, 12):
            stale_second(m, i).wait_send()

    def drain_late(m):
        for i in range(24):
            sum_copy(m, i).wait_send()

        @pl.when(even)
        def _():
            for i in range(13):
                next_copy(m, i).wait_send()

        @pl.when(sec < sections - 1)
        def _():
            for c in range(4):
                hand_on(m, c).wait_send()

    def patch(m, _):
        opening = jnp.logical_and(sec == 0, m == 0)

        @pl.when(even)
        def _():
            await_turn(m)
            modulate_and_send(m)

        @pl.when(opening)
        def _():
            w_copies[0].wait()
            for copy in w_copies[1:]:
                copy.start()
            stale_send(0)

        gather_forward(m)

        @pl.when(opening)
        def _():
            for copy in w_copies[1:5] + v_copies[3:6]:
                copy.wait()
            lax.fori_loop(0, 12, merge, 0)
            stale_forward(0)

        @pl.when(odd)
        def _():
            own_landed(m)

        project(m, 0, EARLY)()
        for i in range(6, 12):
            stale_second_landed(m, i)
        early = attend_cached(m, 0, EARLY)
        gather_rest(m)

        @pl.when(opening)
        def _():
            lax.fori_loop(1, patches, stale_send_step, 0)

        feed = project(m, EARLY, 256)
        late = attend_cached(m, EARLY, 256)
        feed()
        attend_fresh(early, late)

        @pl.when(m == 0)
        def _():
            for copy in w_copies[5:]:
                copy.wait()

        output_products(m)

        @pl.when(opening)
        def _():
            lax.fori_loop(1, patches, stale_forward_step, 0)

        drain_early(m)

        @pl.when(m > 0)
        def _():
            drain_late(m - 1)

        sum_up(m)
        return 0

    lax.fori_loop(0, patches, patch, 0)

    drain_late(patches - 1)

    @pl.when(odd)
    def _():
        for i in range(2):
            modulation_copy(i).wait_send()


def per_device(
    latents, patch_numbers, prior_step_cache, old_block_index, modulation_offset, modulation_scale,
    modulation_gate, query_key_value_weight, feedforward_input_weight, adapter_down_weight,
    adapter_up_query_key_value, adapter_up_feedforward, attention_output_weight,
    feedforward_output_weight,
):
    patches = old_block_index.shape[1]
    vmem = pl.BlockSpec(memory_space=pltpu.VMEM)
    smem = pl.BlockSpec(memory_space=pltpu.SMEM)
    hbm = pl.BlockSpec(memory_space=pl.ANY)
    dma = pltpu.SemaphoreType.DMA
    record = pl.pallas_call(
        kernel,
        out_shape=jax.ShapeDtypeStruct((patches, 16, 3072), BF16),
        in_specs=[smem, smem] + [hbm] * 12,
        out_specs=vmem,
        scratch_shapes=[
            pltpu.VMEM(latents.shape, BF16),
            pltpu.VMEM((1, 3072), F32),
            pltpu.VMEM((1, 3072), F32),
            pltpu.VMEM((1, 3072), F32),
            pltpu.VMEM((3, 64, DH), BF16),
            pltpu.VMEM((64, 768), BF16),
            pltpu.VMEM((64, 3072), BF16),
            pltpu.VMEM((1, 3072), F32),
            pltpu.VMEM((1, 3072), F32),
            pltpu.VMEM((patches, 2, 16, 1536), BF16),
            pltpu.VMEM((3072, 1152), BF16),
            pltpu.VMEM((896, 3072), BF16),
            pltpu.VMEM((16, 16, 2, 2048), BF16),
            pltpu.VMEM((patches, 2, 4, 4, 64, DH), BF16),
            pltpu.VMEM((patches, 2, 4, 4, 64, DH), BF16),
            pltpu.VMEM((patches, 2, 4, 4, 64, DH), BF16),
            pltpu.VMEM((patches, 16, 3072), BF16),
            pltpu.VMEM((patches, 2, 16, 16, 1536), BF16),
            pltpu.VMEM((256, 3 * DH), F32),
            pltpu.VMEM((256, 896), BF16),
            pltpu.VMEM((patches, 4, 4, 4, 16, 768), BF16),
            pltpu.VMEM((patches, 12, 4, 16, 768), BF16),
            pltpu.VMEM((patches, 4, 4, 16, 768), BF16),
            pltpu.VMEM((patches, 12, 16, 768), BF16),
            dma((patches, len(GATHER))),
            dma((patches, len(GATHER) + 1)),
            dma((patches, 24)),
            dma((patches, 24)),
            dma((patches, 12)),
            dma((patches, 12)),
            dma((patches, 4)),
            dma((patches, 4)),
            dma((14,)),
            pltpu.SemaphoreType.REGULAR,
            dma((patches, 13)),
            dma((2,)),
            dma((2,)),
        ],
        compiler_params=pltpu.CompilerParams(
            collective_id=0, has_side_effects=True, vmem_limit_bytes=58 * 2**20
        ),
        cost_estimate=pl.CostEstimate(
            flops=10_000_000_000, bytes_accessed=16_000_000, transcendentals=2_000_000
        ),
    )(
        patch_numbers,
        old_block_index.transpose(1, 0, 2),
        latents,
        modulation_offset,
        modulation_scale,
        modulation_gate,
        adapter_up_query_key_value[0].transpose(1, 0, 2),
        adapter_up_feedforward[0],
        adapter_down_weight[0].T,
        prior_step_cache[0],
        query_key_value_weight[0].transpose(1, 0, 2),
        feedforward_input_weight[0],
        attention_output_weight[0],
        feedforward_output_weight[0],
    )
    return record[None]


def solution(mesh):
    placed = (
        P(None, "head", None),
        P(),
        P("section", None, "head", None, None),
        P("section", None, None),
        P("section", None),
        P("section", None),
        P("section", None),
        P("section", None, None, "head"),
        P("section", None, "head"),
        P("section", None, None),
        P("section", None, None, "head"),
        P("section", None, "head"),
        P("section", "head", None),
        P("section", "head", None),
    )
    return jax.shard_map(
        per_device,
        mesh=mesh,
        in_specs=placed,
        out_specs=P("section", None, "head", None),
        check_vma=False,
    )
```

```python
import math

import jax
import jax.numpy as jnp
from jax import lax
from jax.experimental import pallas as pl
from jax.experimental.pallas import tpu as pltpu
from jax.sharding import PartitionSpec as P

DH = 128
MESH = pl.DeviceIdType.MESH
F32 = jnp.float32
BF16 = jnp.bfloat16
A, B = 0, 1

ORDER = [
    (0, 0), (1, 0), (3, 0), (2, 0), (0, 1), (0, 3), (0, 2),
    (1, 1), (1, 3), (3, 1), (3, 3), (1, 2), (3, 2), (2, 1), (2, 3), (2, 2),
]
EARLY = 7 * 16
FAR_FIRST = (2, 1, 3)
NEAR_FIRST = (1, 3, 2)


def along(axis, d):
    return (d, 0) if axis == 0 else (0, d)


def slot(place):
    return ORDER.index((place[0] % 4, place[1] % 4))


GATHER = []
for axis in (0, 1):
    GATHER += [(axis, (0, 0), along(axis, d)) for d in FAR_FIRST]
for axis in (0, 1):
    GATHER += [(1 - axis, (0, 0), along(axis, d)) for d in FAR_FIRST]
FORWARD = []
for d in NEAR_FIRST:
    for axis in (0, 1):
        first = GATHER.index((axis, (0, 0), along(axis, d)))
        after = [(axis, along(axis, -d % 4), along(1 - axis, e)) for e in FAR_FIRST]
        FORWARD.append((first, range(len(GATHER), len(GATHER) + 3)))
        GATHER += after


def rms_unit(values):
    return values * lax.rsqrt(jnp.mean(values * values, axis=-1, keepdims=True) + 1e-06)


def kernel(
    pn, bidx, lat_hbm, off_hbm, scl_hbm, gate_hbm, upq_hbm, upf_hbm, dnt_hbm, cache_hbm, wqkv_hbm,
    wffn_hbm, woa_hbm, wof_hbm,
    out,
    lat, off, scl, gate, upq, upf, dnt, next_off, next_scl, ahead,
    win, wout, cachev, skv, r1, kv, xin, xg, qkv, act, part, rb, tb, r2,
    ag_s, ag_r, rs_s, rs_r, st_s, st_r, x_s, x_r, w_sem, turn, nx_s, nm_s, nm_r,
):
    patches = xin.shape[0]
    sections = lax.axis_size("section")
    sec = lax.axis_index("section")
    head = lax.axis_index("head")
    x = head // 4
    y = lax.rem(head, 4)

    def px(d):
        return lax.rem(x + (d + 4), 4)

    def py(d):
        return lax.rem(y + (d + 4), 4)

    def dev(d):
        return (sec, px(d[0]) * 4 + py(d[1]))

    first_section = sec == 0
    even = lax.rem(sec, 2) == 0
    odd = lax.rem(sec, 2) == 1

    w_copies = [
        pltpu.make_async_copy(cache_hbm, cachev, w_sem.at[0]),
        pltpu.make_async_copy(wqkv_hbm.at[0], win.at[:, pl.ds(0, DH)], w_sem.at[1]),
        pltpu.make_async_copy(wqkv_hbm.at[1], win.at[:, pl.ds(DH, DH)], w_sem.at[2]),
        pltpu.make_async_copy(wqkv_hbm.at[2], win.at[:, pl.ds(2 * DH, DH)], w_sem.at[3]),
        pltpu.make_async_copy(wffn_hbm, win.at[:, pl.ds(3 * DH, 768)], w_sem.at[4]),
        pltpu.make_async_copy(woa_hbm, wout.at[pl.ds(0, DH)], w_sem.at[5]),
        pltpu.make_async_copy(wof_hbm, wout.at[pl.ds(DH, 768)], w_sem.at[6]),
    ]
    v_copies = [
        pltpu.make_async_copy(source, target, w_sem.at[7 + i])
        for i, (source, target) in enumerate((
            (off_hbm, off), (scl_hbm, scl), (gate_hbm, gate), (upq_hbm, upq), (upf_hbm, upf),
            (dnt_hbm, dnt), (lat_hbm, lat),
        ))
    ]

    @pl.when(first_section)
    def _():
        v_copies[6].start()

    for copy in v_copies[:3]:
        copy.start()
    w_copies[0].start()
    for copy in v_copies[3:6]:
        copy.start()

    barrier = pltpu.get_barrier_semaphore()
    for d in FAR_FIRST:
        for axis in (0, 1):
            pl.semaphore_signal(
                barrier, inc=1, device_id=dev(along(axis, d)), device_id_type=MESH
            )
    for step in (1, sections - 1):
        neighbour = (lax.rem(sec + step, sections), head)
        pl.semaphore_signal(barrier, inc=1, device_id=neighbour, device_id_type=MESH)

    @pl.when(odd)
    def _():
        for d in FAR_FIRST:
            for axis in (0, 1):
                way = along(axis, d)
                peer = (sec - 1, px(way[0]) * 4 + py(way[1]))
                pl.semaphore_signal(barrier, inc=1, device_id=peer, device_id_type=MESH)

    pl.semaphore_wait(barrier, jnp.where(even, 14, 8))

    def remote(src, dst, ssem, rsem, device):
        return pltpu.make_async_remote_copy(
            src_ref=src, dst_ref=dst, send_sem=ssem, recv_sem=rsem, device_id=device,
            device_id_type=MESH,
        )

    def gather_copy(m, i):
        hf, place, way = GATHER[i]
        there = slot((place[0] - way[0], place[1] - way[1]))
        return remote(
            xg.at[m, hf, slot(place)], xg.at[m, hf, there], ag_s.at[m, i], ag_r.at[m, i], dev(way)
        )

    def next_copy(m, i):
        if i == 12:
            return remote(
                ahead.at[m], xg.at[m, :, 0], nx_s.at[m, 12], ag_r.at[m, len(GATHER)], (sec + 1, head)
            )
        hf, _, way = GATHER[i]
        there = slot((-way[0], -way[1]))
        target = (sec + 1, px(way[0]) * 4 + py(way[1]))
        return remote(
            ahead.at[m, hf], xg.at[m, hf, there], nx_s.at[m, i], ag_r.at[m, i], target
        )

    def own_landed(m):
        ref = xg.at[m, :, 0]
        remote(ref, ref, nx_s.at[m, 12], ag_r.at[m, len(GATHER)], (sec - 1, head)).wait_recv()

    def modulation_copy(i):
        source, target = ((off, next_off), (scl, next_scl))[i]
        return remote(source, target, nm_s.at[i], nm_r.at[i], (sec - 1, head))

    def gather_landed(m, i):
        hf, place, way = GATHER[i]
        ref = xg.at[m, hf, slot((place[0] - way[0], place[1] - way[1]))]
        remote(ref, ref, ag_s.at[m, i], ag_r.at[m, i], dev((-way[0], -way[1]))).wait_recv()

    def stale_first(m, i):
        if i < 3:
            d = (1, -1, 2)[i]
            return remote(
                skv.at[m, 0, px(d)], r1.at[m, 0, x], st_s.at[m, i], st_r.at[m, i], dev((d, 0))
            )
        d = (1, -1, 2)[i - 3]
        return remote(
            skv.at[m, 1, py(d)], r1.at[m, 1, y], st_s.at[m, i], st_r.at[m, i], dev((0, d))
        )

    def stale_first_landed(m, i):
        if i < 3:
            d = (-1, 1, 2)[i]
            ref, device = r1.at[m, 0, px(d)], dev((d, 0))
        else:
            d = (-1, 1, 2)[i - 3]
            ref, device = r1.at[m, 1, py(d)], dev((0, d))
        remote(ref, ref, st_s.at[m, i], st_r.at[m, i], device).wait_recv()

    def stale_second(m, i):
        if i < 9:
            d = (1, -1, 2)[i - 6]
            return remote(
                r1.at[m, 0, :, py(d)], kv.at[m, 0, y], st_s.at[m, i], st_r.at[m, i], dev((0, d))
            )
        d = (1, -1, 2)[i - 9]
        return remote(
            r1.at[m, 1, :, px(d)], kv.at[m, 1, x], st_s.at[m, i], st_r.at[m, i], dev((d, 0))
        )

    def stale_second_landed(m, i):
        if i < 9:
            d = (-1, 1, 2)[i - 6]
            ref, device = kv.at[m, 0, py(d)], dev((0, d))
        else:
            d = (-1, 1, 2)[i - 9]
            ref, device = kv.at[m, 1, px(d)], dev((d, 0))
        remote(ref, ref, st_s.at[m, i], st_r.at[m, i], device).wait_recv()

    def stale_send(m):
        def one(j, _):
            block = bidx[m, 0, j]
            both = cachev[block]
            keys = both[:, 0].astype(F32)
            values = both[:, 1]
            rows = pl.ds(pl.multiple_of(j * 16, 16), 16)
            for h in range(16):
                part_k = keys[:, h * DH:(h + 1) * DH]
                skv[m, 0, h // 4, h % 4, rows, :] = rms_unit(part_k).astype(BF16)
                skv[m, 1, h % 4, h // 4, rows, :] = values[:, h * DH:(h + 1) * DH]
            return 0

        lax.fori_loop(0, 4, one, 0)
        for i in range(6):
            stale_first(m, i).start()
        r1[m, 0, x] = skv[m, 0, x]
        r1[m, 1, y] = skv[m, 1, y]

    def stale_forward(m):
        for i in range(3):
            stale_first_landed(m, i)
        for i in range(6, 9):
            stale_second(m, i).start()
        for i in range(3, 6):
            stale_first_landed(m, i)
        for i in range(9, 12):
            stale_second(m, i).start()
        kv[m, 0, y] = r1[m, 0, :, y]
        kv[m, 1, x] = r1[m, 1, :, x]

    def sum_way(i):
        second, c, d = i // 12, i % 12 // 3, FAR_FIRST[i % 3]
        return c, d, along((1 - c % 2) if second == 0 else c % 2, d)

    def sum_copy(m, i):
        c, d, way = sum_way(i)
        if i < 12:
            source = part.at[m, c, :, d] if c % 2 == 0 else part.at[m, c, d]
            target = rb.at[m, i]
        else:
            source, target = tb.at[m, c, d], r2.at[m, i - 12]
        return remote(source, target, rs_s.at[m, i], rs_r.at[m, i], dev(way))

    def sum_landed(m, i):
        _, _, way = sum_way(i)
        target = rb.at[m, i] if i < 12 else r2.at[m, i - 12]
        remote(
            target, target, rs_s.at[m, i], rs_r.at[m, i], dev((-way[0], -way[1]))
        ).wait_recv()

    def hand_on(m, c):
        cols = pl.ds(c * 768, 768)
        return remote(
            out.at[m, :, cols], xin.at[m, :, cols], x_s.at[m, c], x_r.at[m, c], (sec + 1, head)
        )

    def handed(m, c):
        ref = xin.at[m, :, pl.ds(c * 768, 768)]
        remote(ref, ref, x_s.at[m, c], x_r.at[m, c], (sec - 1, head)).wait_recv()

    def modulated(rows, scale, offset):
        values = rows.astype(F32)
        center = values - jnp.mean(values, axis=-1, keepdims=True)
        spread = jnp.mean(center * center, axis=-1, keepdims=True)
        normed = center * lax.rsqrt(spread + 1e-06)
        return (normed * (1.0 + scale[...]) + offset[...]).astype(BF16)

    def modulate_and_send(m):
        @pl.when(first_section)
        def _():
            xin[m] = lat[pn[m]]

        @pl.when(sec > 0)
        def _():
            for c in range(4):
                handed(m, c)

        modded = modulated(xin[m], scl, off)
        xg[m, A, 0] = modded[:, :1536]
        xg[m, B, 0] = modded[:, 1536:]
        for i in range(12):
            gather_copy(m, i).start()

    def gather_forward(m):
        for first, after in FORWARD:
            gather_landed(m, first)
            for i in after:
                gather_copy(m, i).start()
        for i in range(6, 12):
            gather_landed(m, i)

    def gather_rest(m):
        for i in range(12, len(GATHER)):
            gather_landed(m, i)

    def dot(a, b):
        return jnp.dot(a, b, preferred_element_type=F32)

    def dot_tn(a, b):
        return lax.dot_general(a, b, (((0,), (0,)), ((), ())), preferred_element_type=F32)

    def dot_nt(a, b):
        return lax.dot_general(a, b, (((1,), (1,)), ((), ())), preferred_element_type=F32)

    def merge(i, _):
        rows = pl.ds(pl.multiple_of(i * 256, 256), 256)
        down = dnt[:, rows]
        for n in range(3):
            win[rows, n * DH:(n + 1) * DH] = (
                win[rows, n * DH:(n + 1) * DH].astype(F32) + dot_tn(down, upq[n])
            ).astype(BF16)
            cols = slice(3 * DH + n * 256, 3 * DH + (n + 1) * 256)
            win[rows, cols] = (
                win[rows, cols].astype(F32) + dot_tn(down, upf[:, n * 256:(n + 1) * 256])
            ).astype(BF16)
        return 0

    def project(m, lo, hi):
        def tile(first, width):
            acc = None
            for hf in range(2):
                rows = xg[m, hf, lo // 16:hi // 16].reshape(hi - lo, 1536)
                term = dot(rows, win[hf * 1536:(hf + 1) * 1536, pl.ds(first, width)])
                acc = term if acc is None else acc + term
            return acc

        qkv[lo:hi, 0:256] = tile(0, 256)
        qkv[lo:hi, 256:384] = tile(256, DH)

        def feed():
            for n in range(3):
                acc = tile(n * 256 + 3 * DH, 256)
                cols = slice(n * 256 + DH, (n + 1) * 256 + DH)
                act[lo:hi, cols] = jax.nn.gelu(acc, approximate=True).astype(BF16)

        return feed

    def attend_to(queries, keys, values, state):
        expo = jnp.exp(dot_nt(queries, keys) * (1.0 / math.sqrt(DH)))
        total = jnp.sum(expo, axis=-1, keepdims=True)
        mixed = dot(expo.astype(BF16), values)
        return (mixed, total) if state is None else (state[0] + mixed, state[1] + total)

    def attend_cached(m, lo, hi):
        queries = rms_unit(qkv[lo:hi, 0:DH]).astype(BF16)
        state = None
        for j in range(4):
            keys = kv[m, 0, j].reshape(256, DH)
            values = kv[m, 1, :, j].reshape(256, DH)
            state = attend_to(queries, keys, values, state)
        return queries, state

    def attend_fresh(early, late):
        keys = rms_unit(qkv[:, DH:2 * DH]).astype(BF16)
        values = qkv[:, 2 * DH:3 * DH].astype(BF16)
        for lo, hi, (queries, state) in ((0, EARLY, early), (EARLY, 256, late)):
            mixed, total = attend_to(queries, keys, values, state)
            act[lo:hi, 0:DH] = (mixed / total).astype(BF16)

    def output_products(m):
        for c in range(4):
            for n in range(3):
                lo = c * 768 + n * 256
                term = dot(act[...], wout[:, lo:lo + 256]).astype(BF16)
                for k, place in enumerate(ORDER):
                    rows = term[k * 16:(k + 1) * 16]
                    part[m, c, place[0], place[1], :, n * 256:(n + 1) * 256] = rows
            for j in range(3):
                sum_copy(m, 3 * c + j).start()

    def wide(value):
        return value.astype(F32)

    def sum_up(m):
        for c in range(4):
            total = wide(part[m, c, :, 0] if c % 2 == 0 else part[m, c, 0])
            for j in range(3):
                sum_landed(m, 3 * c + j)
                total += wide(rb[m, 3 * c + j])
            tb[m, c] = total.astype(BF16)
            for j in range(3):
                sum_copy(m, 12 + 3 * c + j).start()
        @pl.when(odd)
        def _():
            for c in range(4):
                handed(m, c)

        for c in range(4):
            branch = wide(part[m, c, 0, 0])
            for j in range(3):
                branch += wide(rb[m, 3 * c + j, 0])
            for j in range(3):
                sum_landed(m, 12 + 3 * c + j)
                branch += wide(r2[m, 3 * c + j])
            cols = slice(c * 768, (c + 1) * 768)
            out[m, :, cols] = (wide(xin[m, :, cols]) + gate[:, cols] * branch).astype(BF16)

            @pl.when(jnp.logical_and(odd, sec < sections - 1))
            def _():
                hand_on(m, c).start()

        @pl.when(even)
        def _():
            @pl.when(m == 0)
            def _():
                for i in range(2):
                    source = (next_off, next_scl)[i]
                    remote(
                        source, source, nm_s.at[i], nm_r.at[i], (sec + 1, head)
                    ).wait_recv()

            modded = modulated(out[m], next_scl, next_off)
            ahead[m, A] = modded[:, :1536]
            ahead[m, B] = modded[:, 1536:]
            for i in range(13):
                next_copy(m, i).start()
            for c in range(4):
                hand_on(m, c).start()

    def stale_send_step(m, _):
        stale_send(m)
        return 0

    def stale_forward_step(m, _):
        stale_forward(m)
        return 0

    for copy in v_copies[:3]:
        copy.wait()

    @pl.when(odd)
    def _():
        for i in range(2):
            modulation_copy(i).start()

    @pl.when(sec > 0)
    def _():
        w_copies[0].wait()
        for copy in w_copies[1:]:
            copy.start()
        lax.fori_loop(0, patches, stale_send_step, 0)
        for copy in w_copies[1:5] + v_copies[3:6]:
            copy.wait()
        lax.fori_loop(0, 12, merge, 0)
        lax.fori_loop(0, patches, stale_forward_step, 0)

    @pl.when(first_section)
    def _():
        v_copies[6].wait()

    def await_turn(m):
        @pl.when(m > 0)
        def _():
            pl.semaphore_wait(turn, 1)

    def give_turn(m):
        @pl.when(jnp.logical_and(lax.rem(sec, 2) == 1, m < patches - 1))
        def _():
            pl.semaphore_signal(turn, inc=1, device_id=(sec - 1, head), device_id_type=MESH)

    def patch(m, _):
        opening = jnp.logical_and(sec == 0, m == 0)

        @pl.when(even)
        def _():
            await_turn(m)
            modulate_and_send(m)

        @pl.when(opening)
        def _():
            w_copies[0].wait()
            for copy in w_copies[1:]:
                copy.start()
            stale_send(0)

        gather_forward(m)
        give_turn(m)

        @pl.when(opening)
        def _():
            for copy in w_copies[1:5] + v_copies[3:6]:
                copy.wait()
            lax.fori_loop(0, 12, merge, 0)
            stale_forward(0)

        @pl.when(odd)
        def _():
            own_landed(m)

        project(m, 0, EARLY)()
        for i in range(6, 12):
            stale_second_landed(m, i)
        early = attend_cached(m, 0, EARLY)
        gather_rest(m)

        @pl.when(opening)
        def _():
            lax.fori_loop(1, patches, stale_send_step, 0)

        feed = project(m, EARLY, 256)
        late = attend_cached(m, EARLY, 256)
        feed()
        attend_fresh(early, late)

        @pl.when(m == 0)
        def _():
            for copy in w_copies[5:]:
                copy.wait()

        output_products(m)

        @pl.when(opening)
        def _():
            lax.fori_loop(1, patches, stale_forward_step, 0)

        sum_up(m)
        return 0

    lax.fori_loop(0, patches, patch, 0)

    def drain(m, _):
        @pl.when(even)
        def _():
            for i in range(12):
                gather_copy(m, i).wait_send()
            for i in range(13):
                next_copy(m, i).wait_send()

        for i in range(12, len(GATHER)):
            gather_copy(m, i).wait_send()
        for i in range(24):
            sum_copy(m, i).wait_send()
        for i in range(6):
            stale_first(m, i).wait_send()
        for i in range(6, 12):
            stale_second(m, i).wait_send()

        @pl.when(sec < sections - 1)
        def _():
            for c in range(4):
                hand_on(m, c).wait_send()

        return 0

    lax.fori_loop(0, patches, drain, 0)

    @pl.when(odd)
    def _():
        for i in range(2):
            modulation_copy(i).wait_send()


def per_device(
    latents, patch_numbers, prior_step_cache, old_block_index, modulation_offset, modulation_scale,
    modulation_gate, query_key_value_weight, feedforward_input_weight, adapter_down_weight,
    adapter_up_query_key_value, adapter_up_feedforward, attention_output_weight,
    feedforward_output_weight,
):
    patches = old_block_index.shape[1]
    vmem = pl.BlockSpec(memory_space=pltpu.VMEM)
    smem = pl.BlockSpec(memory_space=pltpu.SMEM)
    hbm = pl.BlockSpec(memory_space=pl.ANY)
    dma = pltpu.SemaphoreType.DMA
    record = pl.pallas_call(
        kernel,
        out_shape=jax.ShapeDtypeStruct((patches, 16, 3072), BF16),
        in_specs=[smem, smem] + [hbm] * 12,
        out_specs=vmem,
        scratch_shapes=[
            pltpu.VMEM(latents.shape, BF16),
            pltpu.VMEM((1, 3072), F32),
            pltpu.VMEM((1, 3072), F32),
            pltpu.VMEM((1, 3072), F32),
            pltpu.VMEM((3, 64, DH), BF16),
            pltpu.VMEM((64, 768), BF16),
            pltpu.VMEM((64, 3072), BF16),
            pltpu.VMEM((1, 3072), F32),
            pltpu.VMEM((1, 3072), F32),
            pltpu.VMEM((patches, 2, 16, 1536), BF16),
            pltpu.VMEM((3072, 1152), BF16),
            pltpu.VMEM((896, 3072), BF16),
            pltpu.VMEM((16, 16, 2, 2048), BF16),
            pltpu.VMEM((patches, 2, 4, 4, 64, DH), BF16),
            pltpu.VMEM((patches, 2, 4, 4, 64, DH), BF16),
            pltpu.VMEM((patches, 2, 4, 4, 64, DH), BF16),
            pltpu.VMEM((patches, 16, 3072), BF16),
            pltpu.VMEM((patches, 2, 16, 16, 1536), BF16),
            pltpu.VMEM((256, 3 * DH), F32),
            pltpu.VMEM((256, 896), BF16),
            pltpu.VMEM((patches, 4, 4, 4, 16, 768), BF16),
            pltpu.VMEM((patches, 12, 4, 16, 768), BF16),
            pltpu.VMEM((patches, 4, 4, 16, 768), BF16),
            pltpu.VMEM((patches, 12, 16, 768), BF16),
            dma((patches, len(GATHER))),
            dma((patches, len(GATHER) + 1)),
            dma((patches, 24)),
            dma((patches, 24)),
            dma((patches, 12)),
            dma((patches, 12)),
            dma((patches, 4)),
            dma((patches, 4)),
            dma((14,)),
            pltpu.SemaphoreType.REGULAR,
            dma((patches, 13)),
            dma((2,)),
            dma((2,)),
        ],
        compiler_params=pltpu.CompilerParams(
            collective_id=0, has_side_effects=True, vmem_limit_bytes=58 * 2**20
        ),
        cost_estimate=pl.CostEstimate(
            flops=10_000_000_000, bytes_accessed=16_000_000, transcendentals=2_000_000
        ),
    )(
        patch_numbers,
        old_block_index.transpose(1, 0, 2),
        latents,
        modulation_offset,
        modulation_scale,
        modulation_gate,
        adapter_up_query_key_value[0].transpose(1, 0, 2),
        adapter_up_feedforward[0],
        adapter_down_weight[0].T,
        prior_step_cache[0],
        query_key_value_weight[0].transpose(1, 0, 2),
        feedforward_input_weight[0],
        attention_output_weight[0],
        feedforward_output_weight[0],
    )
    return record[None]


def solution(mesh):
    placed = (
        P(None, "head", None),
        P(),
        P("section", None, "head", None, None),
        P("section", None, None),
        P("section", None),
        P("section", None),
        P("section", None),
        P("section", None, None, "head"),
        P("section", None, "head"),
        P("section", None, None),
        P("section", None, None, "head"),
        P("section", None, "head"),
        P("section", "head", None),
        P("section", "head", None),
    )
    return jax.shard_map(
        per_device,
        mesh=mesh,
        in_specs=placed,
        out_specs=P("section", None, "head", None),
        check_vma=False,
    )
```
